512 devices in a mesh: tm: 16 (over x, y_lo, core), slab: 32 (over y_hi, z).
Axes of the slice: x: 4, y: 8 (y_hi: 4, y_lo: 2; y = y_hi * 2 + y_lo), z: 8, core: 2. Of those that a mesh axis runs over, the one named last changes fastest.
Arguments:
- slice_starts: float32 [16, 2, 128, 16, 512], P('tm', None, 'slab'), may hold values from 0 to 1
- class_map: int32 [128, 16, 512], P('slab'), may hold values from 0 to 3
- table: float32 [4, 2], replicated, may hold values from 0.03 to 0.16
Outputs:
- final_states: float32 [16, 2, 128, 16, 512], P('tm', None, 'slab')
The draws below stay inside these ranges and needn't reach their ends.
All inputs are finite; a program needn't handle non-finite values.
Results may differ from the reference program's by a relative error of at most 0.000071.
Values sent between devices are 32-bit elements; how exact they have to be, the bound alone decides.
A program may use at most 64 MiB of HBM per device.

```python
import math
import jax
import jax.numpy as jnp

NX = 512
NY = 16
FINE = 4
ITERS = 2
CLASSES = 4
NTS = 16
NZ = 128


def with_ends(values, rng, least, top_value):
    dims = values.shape
    index_at = [jax.random.randint(jax.random.fold_in(rng, axis), (), 0, dims[axis]) for axis in range(len(dims))]
    values = values.at[tuple(index_at)].set(least)
    longest = dims.index(max(dims))
    index_at[longest] = (index_at[longest] + 1) % dims[longest]
    return values.at[tuple(index_at)].set(top_value)


def block_scale(key, shape, split, low, largest):
    factor_of, own = 1.0, jax.random.fold_in(key, 6)
    for position, parts in split:
        heights = jnp.exp(jax.random.uniform(jax.random.fold_in(own, position), (parts,), jnp.float32, low / len(split), largest / len(split)))
        factor_of = factor_of * jnp.repeat(heights, shape[position] // parts).reshape([-1 if axis == position else 1 for axis in range(len(shape))])
    return factor_of


def setup_inputs(seed: int = 0) -> dict:
    splits = jax.random.split(jax.random.key(seed), 4)
    slice_starts = jnp.clip(1.0 * jax.random.uniform(splits[0], (NTS, 2, NZ, NY, NX), jnp.float32) ** block_scale(splits[0], (NTS, 2, NZ, NY, NX), ((0, 16), (2, 32)), -0.2, 0.2), 0.0, 1.0)
    class_map = with_ends(jax.random.randint(splits[1], (NZ, NY, NX), 0, CLASSES), jax.random.fold_in(splits[1], 1), 0, CLASSES - 1).astype(jnp.int32)
    table = jnp.clip(jnp.exp(jax.random.uniform(splits[2], (CLASSES, 2), jnp.float32, math.log(0.03), math.log(0.16))), 0.03, 0.16)
    return {"slice_starts": slice_starts, "class_map": class_map, "table": table}


FEED = 0.04
KILL = 0.062
STEP = 0.04


def reaction(field):
    u_part = field[0]
    v_part = field[1]
    uvv = u_part * v_part * v_part
    return jnp.stack([-uvv + FEED * (1.0 - u_part), uvv - (FEED + KILL) * v_part])


def inplane(field):
    return jnp.roll(field, 1, -1) + jnp.roll(field, -1, -1) + jnp.roll(field, 1, -2) + jnp.roll(field, -1, -2)


def coefficients(class_map, table):
    lam = jnp.zeros((2,) + class_map.shape, jnp.float32)
    for klass in range(CLASSES):
        lam = lam + jnp.where(class_map[None] == klass, table[klass][:, None, None, None], jnp.float32(0.0))
    return lam


def fine_prop(field, lam):
    for step in range(FINE):
        vertical = jnp.roll(field, -1, 1) + jnp.roll(field, 1, 1)
        lap = vertical + inplane(field) - 6.0 * field
        field = field + lam * lap + STEP * reaction(field)
    return field


def coarse_prop(field, coarse_lam):
    return field + coarse_lam * (inplane(field) - 4.0 * field) + (FINE * STEP) * reaction(field)


def reference(slice_starts, class_map, table):
    lam = coefficients(class_map, table)
    coarse_lam = FINE * lam / (1.0 + 4.0 * FINE * lam)
    guess = [slice_starts[j] for j in range(NTS)]
    ends = []
    for sweep in range(ITERS):
        corr = [fine_prop(guess[j], lam) - coarse_prop(guess[j], coarse_lam) for j in range(NTS)]
        starts = [slice_starts[0]]
        ends = []
        for j in range(NTS):
            end_state = coarse_prop(starts[j], coarse_lam) + corr[j]
            ends.append(end_state)
            starts.append(end_state)
        guess = starts[:NTS]
    return jnp.stack(ends)
```

```python
import functools

import jax
import jax.numpy as jnp
from jax import lax
from jax.experimental import pallas as pl
from jax.experimental.pallas import tpu as pltpu
from jax.sharding import PartitionSpec as P

FINE = 4
CLASSES = 4
NTS = 16
FEED = 0.04
KILL = 0.062
STEP = 0.04
PLANES = 4
ROWS = 16
COLS = 512
LANES = 128
CHUNKS = COLS // LANES
HALO = FINE
DEEP = PLANES + 2 * HALO
PIECE = 2 * ROWS + 8
MESH = pl.DeviceIdType.MESH


def react(u, v, scale):
    uvv = u * v * v
    return scale * (FEED * (1.0 - u) - uvv), scale * (uvv - (FEED + KILL) * v)


def four(a):
    rows, cols = a.shape
    return (
        pltpu.roll(a, 1, 1)
        + pltpu.roll(a, cols - 1, 1)
        + pltpu.roll(a, 1, 0)
        + pltpu.roll(a, rows - 1, 0)
    )


def coarse(u, v, cu, cv):
    ru, rv = react(u, v, FINE * STEP)
    return u + cu * (four(u) - 4.0 * u) + ru, v + cv * (four(v) - 4.0 * v) + rv


def coarse_of(lam):
    return FINE * lam / (1.0 + 4.0 * FINE * lam)


def kernel(
    ss, cm_in, table, out,
    lv, cm, lam, gb, pack, got, made,
    load_sem, hs, hr, cs, cr, ps, pr, vs, vr,
):
    t = lax.axis_index("tm")
    s = lax.axis_index("slab")
    slabs = lax.axis_size("slab")
    up = lax.rem(s + 1, slabs)
    down = lax.rem(s + slabs - 1, slabs)
    my_plane = t // CHUNKS
    my_chunk = lax.rem(t, CHUNKS)

    def at_slab(z):
        return (t, z)

    barrier = pltpu.get_barrier_semaphore()
    for z in (up, down):
        pl.semaphore_signal(barrier, inc=1, device_id=at_slab(z), device_id_type=MESH)

    def greet(k, carry):
        peer = lax.rem(t + k, NTS)
        pl.semaphore_signal(barrier, inc=1, device_id=(peer, s), device_id_type=MESH)
        return carry

    lax.fori_loop(1, NTS, greet, 0)

    loads = [
        pltpu.make_async_copy(ss.at[0, :, p], lv.at[0, HALO + p], load_sem.at[p])
        for p in range(PLANES)
    ]
    loads.append(pltpu.make_async_copy(cm_in, cm.at[pl.ds(HALO, PLANES)], load_sem.at[PLANES]))
    for copy in loads:
        copy.start()
    pl.semaphore_wait(barrier, NTS + 1)

    def halo_copies(sweep, i):
        if sweep == 0:
            tail, head = ss.at[0, :, PLANES - 1 - i], ss.at[0, :, i]
        else:
            tail, head = lv.at[4, HALO + PLANES - 1 - i], lv.at[4, HALO + i]
        return [
            pltpu.make_async_remote_copy(
                src_ref=src,
                dst_ref=lv.at[4 * sweep, plane],
                send_sem=hs.at[sweep, way, i],
                recv_sem=hr.at[sweep, way, i],
                device_id=at_slab(z),
                device_id_type=MESH,
            )
            for way, (src, plane, z) in enumerate(
                ((tail, HALO - 1 - i, up), (head, HALO + PLANES + i, down))
            )
        ]

    def class_copies(i):
        return [
            pltpu.make_async_remote_copy(
                src_ref=cm_in.at[src],
                dst_ref=cm.at[plane],
                send_sem=cs.at[way, i],
                recv_sem=cr.at[way, i],
                device_id=at_slab(z),
                device_id_type=MESH,
            )
            for way, (src, plane, z) in enumerate(
                ((PLANES - 1 - i, HALO - 1 - i, up), (i, HALO + PLANES + i, down))
            )
        ]

    for i in range(HALO):
        for copy in halo_copies(0, i):
            copy.start()
        if i < HALO - 1:
            for copy in class_copies(i):
                copy.start()

    def diffusivity(plane):
        klass = cm[plane]
        for field in range(2):
            value = jnp.zeros(klass.shape, jnp.float32)
            for k in range(CLASSES):
                value = jnp.where(klass == k, table[k, field], value)
            lam[plane, field] = value

    for copy in loads:
        copy.wait()

    def own_lam(p, carry):
        diffusivity(HALO + p)
        return carry

    lax.fori_loop(0, PLANES, own_lam, 0)

    def fine(base, level, plane):
        u, v = lv[base + level - 1, plane, 0], lv[base + level - 1, plane, 1]
        lap_u = lv[base + level - 1, plane - 1, 0] + lv[base + level - 1, plane + 1, 0]
        lap_v = lv[base + level - 1, plane - 1, 1] + lv[base + level - 1, plane + 1, 1]
        lap_u = lap_u + four(u) - 6.0 * u
        lap_v = lap_v + four(v) - 6.0 * v
        ru, rv = react(u, v, STEP)
        return u + lam[plane, 0] * lap_u + ru, v + lam[plane, 1] * lap_v + rv

    def fine_group(base, d):
        def step(k, carry):
            low = HALO - d + k
            for plane in (low, DEEP - 1 - low):
                u, v = fine(base, k, plane)
                lv[base + k, plane, 0] = u
                lv[base + k, plane, 1] = v
            return carry

        lax.fori_loop(1, min(d + 1, FINE - 1) + 1, step, 0)

    def guesses(sweep):
        keep = jnp.where(t == sweep, 0.0, 1.0).astype(jnp.float32)

        def one(p, carry):
            q = HALO + p
            cu, cv = coarse_of(lam[q, 0]), coarse_of(lam[q, 1])
            gu, gv = coarse(lv[4 * sweep, q, 0], lv[4 * sweep, q, 1], cu, cv)
            gb[p, 0] = keep * gu
            gb[p, 1] = keep * gv
            return carry

        lax.fori_loop(0, PLANES, one, 0)

    def piece_copy(sweep, owner):
        return pltpu.make_async_remote_copy(
            src_ref=pack.at[sweep, owner],
            dst_ref=got.at[sweep, t],
            send_sem=ps.at[sweep, owner],
            recv_sem=pr.at[sweep, t],
            device_id=(owner, s),
            device_id_type=MESH,
        )

    lane = lax.broadcasted_iota(jnp.int32, (8, LANES), 1)

    def last_step(sweep, q):
        p = q - HALO
        u, v = fine(4 * sweep, FINE, q)
        @pl.when(t == sweep)
        def _():
            out[0, 0, p] = u
            out[0, 1, p] = v
        u = u - gb[p, 0]
        v = v - gb[p, 1]
        for c in range(CHUNKS):
            owner = p * CHUNKS + c
            here = slice(c * LANES, (c + 1) * LANES)
            after = ((c + 1) % CHUNKS) * LANES
            before = ((c - 1) % CHUNKS) * LANES
            pack[sweep, owner, 0:ROWS] = u[:, here]
            pack[sweep, owner, ROWS : 2 * ROWS] = v[:, here]
            edges = None
            for quarter, (field, row) in enumerate(((u, 0), (u, 8), (v, 0), (v, 8))):
                both = jnp.where(
                    lane < 64,
                    field[row : row + 8, after : after + LANES],
                    field[row : row + 8, before : before + LANES],
                )
                both = pltpu.roll(both, 32 * quarter + 16, 1)
                edges = both if edges is None else jnp.where(lane // 32 == quarter, both, edges)
            pack[sweep, owner, 2 * ROWS : PIECE] = edges

        def send(c, carry):
            owner = p * CHUNKS + c

            @pl.when(owner != t)
            def _():
                piece_copy(sweep, owner).start()

            @pl.when(owner == t)
            def _():
                pltpu.make_async_copy(
                    pack.at[sweep, owner], got.at[sweep, t], pr.at[sweep, t]
                ).start()

            return carry

        lax.fori_loop(0, CHUNKS, send, 0)

    def propagate(sweep):
        base = 4 * sweep
        fine_group(base, 0)
        guesses(sweep)
        for d in range(1, HALO + 1):
            for copy in halo_copies(sweep, d - 1):
                copy.wait_recv()
            if sweep == 0 and d >= 2:
                for copy in class_copies(d - 2):
                    copy.wait_recv()
                diffusivity(HALO + 1 - d)
                diffusivity(HALO + PLANES - 2 + d)
            fine_group(base, d)
            if d + 1 >= FINE:
                low = 2 * HALO - d
                last_step(sweep, low)
                last_step(sweep, DEEP - 1 - low)

    def state_copy(sweep, target, src):
        columns = pl.ds(pl.multiple_of(my_chunk * LANES, LANES), LANES)
        if sweep == 0:
            dst = lv.at[4, HALO + my_plane, :, :, columns]
        else:
            dst = out.at[0, :, my_plane, :, columns]
        return (
            pltpu.make_async_remote_copy(
                src_ref=src,
                dst_ref=dst,
                send_sem=vs.at[sweep, target],
                recv_sem=vr.at[sweep, my_plane],
                device_id=(target, s),
                device_id_type=MESH,
            ),
            pltpu.make_async_copy(src, dst, vr.at[sweep, my_plane]),
        )

    def send_state(sweep, target, src):
        remote, local = state_copy(sweep, target, src)

        @pl.when(target != t)
        def _():
            remote.start()

        @pl.when(target == t)
        def _():
            local.start()

    def wait_piece(sweep, j):
        pltpu.make_async_copy(got.at[sweep, j], got.at[sweep, j], pr.at[sweep, j]).wait()

    def unpack(sweep, j):
        edges = got[sweep, j, 2 * ROWS : PIECE]
        parts = [pltpu.roll(edges, LANES - (32 * quarter + 16), 1) for quarter in range(4)]
        fields = []
        for field in range(2):
            side = jnp.concatenate(parts[2 * field : 2 * field + 2], axis=0)
            main = got[sweep, j, field * ROWS : (field + 1) * ROWS]
            fields.append(jnp.concatenate([main, side], axis=1))
        return fields

    def relay(sweep):
        columns = [
            pl.ds(pl.multiple_of(lax.rem(my_chunk + k, CHUNKS) * LANES, LANES), LANES)
            for k in (0, 1, CHUNKS - 1)
        ]
        wide = lax.broadcasted_iota(jnp.int32, (ROWS, LANES), 1)
        maps = []
        for field in range(2):
            here, after, before = [lam[HALO + my_plane, field, :, c] for c in columns]
            both = jnp.concatenate([here, jnp.where(wide < 64, after, before)], axis=1)
            maps.append(coarse_of(both))
        wait_piece(sweep, sweep)
        u, v = unpack(sweep, sweep)
        if sweep == 0:
            made[0, 0, 0] = u[:, :LANES]
            made[0, 0, 1] = v[:, :LANES]
            send_state(0, 1, made.at[0, 0])

        def step(m, carry):
            u, v = carry
            j = m + sweep
            wait_piece(sweep, j)
            cu, cv = unpack(sweep, j)
            u, v = coarse(u, v, maps[0], maps[1])
            u, v = u + cu, v + cv
            made[sweep, m, 0] = u[:, :LANES]
            made[sweep, m, 1] = v[:, :LANES]
            send_state(sweep, m + 1, made.at[sweep, m])
            return u, v

        lax.fori_loop(1, NTS - 1, step, (u, v))

    @pl.when(t < NTS - 1)
    def _():
        propagate(0)

    @pl.when(t == NTS - 1)
    def _():
        for d in range(HALO):
            for copy in halo_copies(0, d):
                copy.wait_recv()
            if d < HALO - 1:
                for copy in class_copies(d):
                    copy.wait_recv()
                diffusivity(HALO - 1 - d)
                diffusivity(HALO + PLANES + d)

    relay(0)

    def wait_plane(sweep, p):
        if sweep == 0:
            ref = lv.at[4, HALO + p]
        else:
            ref = out.at[0, :, p]
        pltpu.make_async_copy(ref, ref, vr.at[sweep, p]).wait()

    @pl.when(t > 0)
    def _():
        for i in range(HALO):
            if i < 2:
                wait_plane(0, PLANES - 1 - i)
                wait_plane(0, i)
            for copy in halo_copies(1, i):
                copy.start()
        propagate(1)

    relay(1)

    @pl.when(t > 1)
    def _():
        for p in range(PLANES):
            wait_plane(1, p)

    for i in range(HALO):
        for copy in halo_copies(0, i):
            copy.wait_send()
        if i < HALO - 1:
            for copy in class_copies(i):
                copy.wait_send()

    @pl.when(t > 0)
    def _():
        for i in range(HALO):
            for copy in halo_copies(1, i):
                copy.wait_send()

    for sweep in range(2):
        sender = t < NTS - 1 if sweep == 0 else t > 0

        def drain(owner, carry):
            @pl.when(sender & (owner != t))
            def _():
                piece_copy(sweep, owner).wait_send()

            @pl.when((owner != t) & (owner > sweep))
            def _():
                state_copy(sweep, owner, made.at[sweep, 0])[0].wait_send()

            return carry

        lax.fori_loop(0, NTS, drain, 0)


def on_device(slice_starts, class_map, table):
    field = (2, ROWS, COLS)
    return pl.pallas_call(
        kernel,
        out_shape=jax.ShapeDtypeStruct(slice_starts.shape, jnp.float32),
        in_specs=[
            pl.BlockSpec(memory_space=pl.ANY),
            pl.BlockSpec(memory_space=pl.ANY),
            pl.BlockSpec(memory_space=pltpu.SMEM),
        ],
        out_specs=pl.BlockSpec(memory_space=pltpu.VMEM),
        scratch_shapes=[
            pltpu.VMEM((2 * FINE, DEEP) + field, jnp.float32),
            pltpu.VMEM((DEEP, ROWS, COLS), jnp.int32),
            pltpu.VMEM((DEEP,) + field, jnp.float32),
            pltpu.VMEM((PLANES,) + field, jnp.float32),
            pltpu.VMEM((2, NTS, PIECE, LANES), jnp.float32),
            pltpu.VMEM((2, NTS, PIECE, LANES), jnp.float32),
            pltpu.VMEM((2, NTS, 2, ROWS, LANES), jnp.float32),
            pltpu.SemaphoreType.DMA((PLANES + 1,)),
            pltpu.SemaphoreType.DMA((2, 2, HALO)),
            pltpu.SemaphoreType.DMA((2, 2, HALO)),
            pltpu.SemaphoreType.DMA((2, HALO - 1)),
            pltpu.SemaphoreType.DMA((2, HALO - 1)),
            pltpu.SemaphoreType.DMA((2, NTS)),
            pltpu.SemaphoreType.DMA((2, NTS)),
            pltpu.SemaphoreType.DMA((2, NTS)),
            pltpu.SemaphoreType.DMA((2, PLANES)),
        ],
        compiler_params=pltpu.CompilerParams(
            collective_id=0, has_side_effects=True, vmem_limit_bytes=32 * 1024 * 1024
        ),
        name="parareal",
    )(slice_starts, class_map, table)


def solution(mesh):
    in_specs = (P("tm", None, "slab", None, None), P("slab", None, None), P())
    out_specs = P("tm", None, "slab", None, None)
    return jax.shard_map(
        on_device, mesh=mesh, in_specs=in_specs, out_specs=out_specs, check_vma=False
    )
```

```python
import functools

import jax
import jax.numpy as jnp
from jax import lax
from jax.experimental import pallas as pl
from jax.experimental.pallas import tpu as pltpu
from jax.sharding import PartitionSpec as P

FINE = 4
CLASSES = 4
NTS = 16
FEED = 0.04
KILL = 0.062
STEP = 0.04
PLANES = 4
ROWS = 16
COLS = 512
LANES = 128
CHUNKS = COLS // LANES
HALO = FINE
DEEP = PLANES + 2 * HALO
PIECE = 2 * ROWS + 8
MESH = pl.DeviceIdType.MESH
TALL = 8
ROUND = ((3, 0), (3, 1), (2, 1))


def react(u, v, scale):
    uvv = u * v * v
    return scale * (FEED * (1.0 - u) - uvv), scale * (uvv - (FEED + KILL) * v)


def four(a):
    rows, cols = a.shape
    return (
        pltpu.roll(a, 1, 1)
        + pltpu.roll(a, cols - 1, 1)
        + pltpu.roll(a, 1, 0)
        + pltpu.roll(a, rows - 1, 0)
    )


def coarse(u, v, cu, cv):
    ru, rv = react(u, v, FINE * STEP)
    return u + cu * (four(u) - 4.0 * u) + ru, v + cv * (four(v) - 4.0 * v) + rv


def coarse_of(lam):
    return FINE * lam / (1.0 + 4.0 * FINE * lam)


def kernel(
    ss, cm_in, table, out,
    lv, cm, lam, gb, pack, got, made, tails, heads, kinds, planes,
    load_sem, hs, hr, ts, tr, ds, dr, cs, cr, xs, xr, ks, kr,
    gs, gr, es, er, fs, ps, pr, vs, vr, ready, here,
):
    t = lax.axis_index("tm")
    s = lax.axis_index("slab")
    slabs = lax.axis_size("slab")
    up = lax.rem(s + 1, slabs)
    down = lax.rem(s + slabs - 1, slabs)
    my_plane = t // CHUNKS
    my_chunk = lax.rem(t, CHUNKS)
    my_columns = pl.ds(pl.multiple_of(my_chunk * LANES, LANES), LANES)
    core = lax.rem(t, 2)
    partner = t + 1 - 2 * core
    last = t == NTS - 1
    height = lax.rem(s, TALL)
    top, bottom = height == TALL - 1, height == 0
    end = top | bottom
    across = jnp.where(top, s - (TALL - 1), jnp.where(bottom, s + (TALL - 1), s))
    beside_up = lax.rem(s + TALL, slabs)
    beside_down = lax.rem(s + slabs - TALL, slabs)
    UP, DOWN = 0, 1

    def signal(sem, where):
        pl.semaphore_signal(sem, inc=1, device_id=where, device_id_type=MESH)

    def remote(src, dst, send, recv, where):
        return pltpu.make_async_remote_copy(
            src_ref=src,
            dst_ref=dst,
            send_sem=send,
            recv_sem=recv,
            device_id=where,
            device_id_type=MESH,
        )

    def arrived(ref, sem):
        pltpu.make_async_copy(ref, ref, sem).wait()

    barrier = pltpu.get_barrier_semaphore()
    signal(barrier, (partner, s))
    signal(barrier, (t, down))

    @pl.when(jnp.logical_not(top))
    def _():
        signal(barrier, (t, up))

    @pl.when(bottom)
    def _():
        for z in (across, beside_up, beside_down):
            signal(barrier, (t, z))

    @pl.when(jnp.logical_not(last | end))
    def _():
        signal(barrier, (NTS - 1, s))

    loads = [
        pltpu.make_async_copy(ss.at[0, :, p], lv.at[0, HALO + p], load_sem.at[p])
        for p in range(PLANES)
    ]
    loads.append(pltpu.make_async_copy(cm_in, cm.at[pl.ds(HALO, PLANES)], load_sem.at[PLANES]))
    for copy in loads:
        copy.start()
    pl.semaphore_wait(barrier, 3 + jnp.where(end, 1, 0) + jnp.where(last, NTS - 1, 0))

    @pl.when(top)
    def _():
        signal(here, (t, up))
        signal(here, (t, across))

        @pl.when(jnp.logical_not(last))
        def _():
            signal(barrier, (NTS - 1, s))

    @pl.when(last)
    def _():
        @pl.when(bottom)
        def _():
            pl.semaphore_wait(here, 2)

        def tell(peer, carry):
            signal(ready, (peer, s))
            return carry

        lax.fori_loop(0, NTS - 1, tell, 0)

    def carrier(way):
        return ((core == way) & (t < NTS - 2)) | (t == NTS - 2)

    def class_planes(way, i):
        return (PLANES - 1 - i, HALO - 1 - i) if way == UP else (i, HALO + PLANES + i)

    def class_copy(way, i):
        src, plane = class_planes(way, i)
        return remote(
            cm_in.at[src], cm.at[plane], cs.at[way, i], cr.at[way, i], (t, down if way else up)
        )

    def kind_copy(i):
        return remote(cm_in.at[i], kinds.at[i], cs.at[DOWN, i], kr.at[i], (t, beside_down))

    def kind_forward(i):
        return remote(
            kinds.at[i], cm.at[HALO + PLANES + i], ks.at[i], cr.at[DOWN, i], (t, across)
        )

    def class_share(way, i):
        plane = class_planes(way, i)[1]
        return remote(cm.at[plane], cm.at[plane], xs.at[way, i], xr.at[way, i], (partner, s))

    def send_class():
        @pl.when(carrier(UP))
        def _():
            for i in range(HALO - 1):
                class_copy(UP, i).start()

        @pl.when(carrier(DOWN) & bottom)
        def _():
            for i in range(HALO - 1):
                kind_copy(i).start()

        @pl.when(carrier(DOWN) & jnp.logical_not(bottom))
        def _():
            for i in range(HALO - 1):
                class_copy(DOWN, i).start()

    def pass_class():
        @pl.when(carrier(DOWN))
        def _():
            for i in range(HALO - 1):
                copy = kind_forward(i)
                kind_copy(i).wait_recv()
                copy.start()

    def share_class():
        for way in (UP, DOWN):

            @pl.when(carrier(way))
            def _():
                for i in range(HALO - 1):
                    share = class_share(way, i)
                    class_copy(way, i).wait_recv()
                    share.start()

    def take_class(i):
        for way in (UP, DOWN):

            @pl.when(jnp.logical_not(carrier(way)))
            def _():
                class_share(way, i).wait_recv()

        diffusivity(HALO - 1 - i)
        diffusivity(HALO + PLANES + i)

    def drain_class():
        for way in (UP, DOWN):

            @pl.when(carrier(way))
            def _():
                for i in range(HALO - 1):
                    class_copy(way, i).wait_send()
                    class_share(way, i).wait_send()

        @pl.when(bottom & carrier(DOWN))
        def _():
            for i in range(HALO - 1):
                kind_forward(i).wait_send()

    def unit_source(way, i, field):
        return ss.at[0, field, PLANES - 1 - i if way == UP else i]

    def unit_target(way, i, field):
        return lv.at[0, HALO - 1 - i if way == UP else HALO + PLANES + i, field]

    def unit_copy(way, i, field):
        return remote(
            unit_source(way, i, field),
            unit_target(way, i, field),
            hs.at[way, i, field],
            hr.at[way, i, field],
            (t, up if way == UP else down),
        )

    def tail_copy(n):
        i, field = ROUND[n]
        return remote(
            unit_source(UP, i, field), tails.at[n], hs.at[UP, i, field], tr.at[n], (t, across)
        )

    def tail_forward(n):
        i, field = ROUND[n]
        return remote(
            tails.at[n], unit_target(UP, i, field), ts.at[n], hr.at[UP, i, field], (t, beside_up)
        )

    def head_copy(i, field):
        return remote(
            unit_source(DOWN, i, field),
            heads.at[i, field],
            hs.at[DOWN, i, field],
            dr.at[i, field],
            (t, beside_down),
        )

    def head_forward(i, field):
        return remote(
            heads.at[i, field],
            unit_target(DOWN, i, field),
            ds.at[i, field],
            hr.at[DOWN, i, field],
            (t, across),
        )

    UNITS = [(i, field) for i in range(HALO) for field in range(2)]

    def send_starts():
        @pl.when(top)
        def _():
            for i, field in UNITS[:2]:
                unit_copy(UP, i, field).start()
            for n in range(len(ROUND)):
                tail_copy(n).start()
            for i, field in UNITS[2:]:
                if (i, field) not in ROUND:
                    unit_copy(UP, i, field).start()
            for i, field in UNITS:
                unit_copy(DOWN, i, field).start()

        @pl.when(bottom)
        def _():
            for i, field in UNITS:
                head_copy(i, field).start()
                unit_copy(UP, i, field).start()

        @pl.when(jnp.logical_not(end))
        def _():
            for i, field in UNITS:
                unit_copy(UP, i, field).start()
                unit_copy(DOWN, i, field).start()

    def pass_heads(units):
        for i, field in units:
            copy = head_forward(i, field)
            head_copy(i, field).wait_recv()
            copy.start()

    def pass_tails():
        for n in range(len(ROUND)):
            copy = tail_forward(n)
            tail_copy(n).wait_recv()
            copy.start()

    def drain_starts():
        for way in (UP, DOWN):
            for i, field in UNITS:
                unit_copy(way, i, field).wait_send()

        @pl.when(bottom)
        def _():
            for i, field in UNITS:
                head_forward(i, field).wait_send()
            for n in range(len(ROUND)):
                tail_forward(n).wait_send()

    def outer(way, i):
        return lv.at[4, HALO - 1 - i if way == UP else HALO + PLANES + i]

    def plane_copy(way, i):
        return remote(
            lv.at[4, HALO + (PLANES - 1 - i if way == UP else i)],
            outer(way, i),
            gs.at[way, i],
            gr.at[way, i],
            (t, up if way == UP else down),
        )

    def send_planes(each):
        for way, over in ((UP, top), (DOWN, bottom)):

            @pl.when(jnp.logical_not(over))
            def _():
                for i in each:
                    plane_copy(way, i).start()

    def plane_forward(i):
        n = i - HALO // 2
        return remote(
            planes.at[n],
            lv.at[4, jnp.where(bottom, HALO - 1 - i, HALO + PLANES + i)],
            fs.at[n],
            gr.at[jnp.where(bottom, UP, DOWN), i],
            (t, jnp.where(bottom, beside_up, beside_down)),
        )

    def pass_planes():
        @pl.when(end)
        def _():
            for i in range(HALO // 2, HALO):
                n = i - HALO // 2
                copy = plane_forward(i)
                arrived(planes.at[n], er.at[n])
                copy.start()

    def drain_planes():
        for way, over in ((UP, top), (DOWN, bottom)):

            @pl.when(jnp.logical_not(over))
            def _():
                for i in range(HALO):
                    plane_copy(way, i).wait_send()

        @pl.when(end)
        def _():
            for i in range(HALO // 2, HALO):
                plane_forward(i).wait_send()

    far = jnp.where(top, PLANES - 1 - my_plane, my_plane)

    def straight_copy(target, src):
        return remote(
            src,
            lv.at[4, jnp.where(top, my_plane, HALO + PLANES + my_plane), :, :, my_columns],
            es.at[target],
            gr.at[jnp.where(top, UP, DOWN), far],
            (target, jnp.where(top, up, down)),
        )

    def round_copy(target, src):
        n = jnp.where(far < HALO // 2, 0, far - HALO // 2)
        return remote(
            src, planes.at[n, :, :, my_columns], es.at[target], er.at[n], (target, across)
        )

    def send_over(target, src):
        @pl.when(end & (far < HALO // 2))
        def _():
            straight_copy(target, src).start()

        @pl.when(end & (far >= HALO // 2))
        def _():
            round_copy(target, src).start()

    def wait_halo(sweep, i):
        for way in (UP, DOWN):
            if sweep == 0:
                for field in range(2):
                    unit_copy(way, i, field).wait_recv()
            else:
                arrived(outer(way, i), gr.at[way, i])

    send_class()

    @pl.when(jnp.logical_not(last))
    def _():
        send_starts()

    def diffusivity(plane):
        klass = cm[plane]
        for field in range(2):
            value = jnp.zeros(klass.shape, jnp.float32)
            for k in range(CLASSES):
                value = jnp.where(klass == k, table[field, k], value)
            lam[plane, field] = value

    for copy in loads:
        copy.wait()

    def own_lam(p, carry):
        diffusivity(HALO + p)
        return carry

    lax.fori_loop(0, PLANES, own_lam, 0)

    def fine(base, level, plane):
        u, v = lv[base + level - 1, plane, 0], lv[base + level - 1, plane, 1]
        lap_u = lv[base + level - 1, plane - 1, 0] + lv[base + level - 1, plane + 1, 0]
        lap_v = lv[base + level - 1, plane - 1, 1] + lv[base + level - 1, plane + 1, 1]
        lap_u = lap_u + four(u) - 6.0 * u
        lap_v = lap_v + four(v) - 6.0 * v
        ru, rv = react(u, v, STEP)
        return u + lam[plane, 0] * lap_u + ru, v + lam[plane, 1] * lap_v + rv

    def fine_group(base, d):
        def step(k, carry):
            low = HALO - d + k
            for plane in (low, DEEP - 1 - low):
                u, v = fine(base, k, plane)
                lv[base + k, plane, 0] = u
                lv[base + k, plane, 1] = v
            return carry

        lax.fori_loop(1, min(d + 1, FINE - 1) + 1, step, 0)

    def guesses(sweep):
        keep = jnp.where(t == sweep, 0.0, 1.0).astype(jnp.float32)

        def one(p, carry):
            q = HALO + p
            cu, cv = coarse_of(lam[q, 0]), coarse_of(lam[q, 1])
            gu, gv = coarse(lv[4 * sweep, q, 0], lv[4 * sweep, q, 1], cu, cv)
            gb[p, 0] = keep * gu
            gb[p, 1] = keep * gv
            return carry

        lax.fori_loop(0, PLANES, one, 0)

    def piece_copy(sweep, owner):
        return pltpu.make_async_remote_copy(
            src_ref=pack.at[sweep, owner],
            dst_ref=got.at[sweep, t],
            send_sem=ps.at[sweep, owner],
            recv_sem=pr.at[sweep, t],
            device_id=(owner, s),
            device_id_type=MESH,
        )

    lane = lax.broadcasted_iota(jnp.int32, (8, LANES), 1)

    def last_step(sweep, q):
        p = q - HALO
        u, v = fine(4 * sweep, FINE, q)
        @pl.when(t == sweep)
        def _():
            out[0, 0, p] = u
            out[0, 1, p] = v
        u = u - gb[p, 0]
        v = v - gb[p, 1]
        for c in range(CHUNKS):
            owner = p * CHUNKS + c
            here = slice(c * LANES, (c + 1) * LANES)
            after = ((c + 1) % CHUNKS) * LANES
            before = ((c - 1) % CHUNKS) * LANES
            pack[sweep, owner, 0:ROWS] = u[:, here]
            pack[sweep, owner, ROWS : 2 * ROWS] = v[:, here]
            edges = None
            for quarter, (field, row) in enumerate(((u, 0), (u, 8), (v, 0), (v, 8))):
                both = jnp.where(
                    lane < 64,
                    field[row : row + 8, after : after + LANES],
                    field[row : row + 8, before : before + LANES],
                )
                both = pltpu.roll(both, 32 * quarter + 16, 1)
                edges = both if edges is None else jnp.where(lane // 32 == quarter, both, edges)
            pack[sweep, owner, 2 * ROWS : PIECE] = edges

        def send(c, carry):
            owner = p * CHUNKS + c

            @pl.when(owner != t)
            def _():
                piece_copy(sweep, owner).start()

            @pl.when(owner == t)
            def _():
                pltpu.make_async_copy(
                    pack.at[sweep, owner], got.at[sweep, t], pr.at[sweep, t]
                ).start()

            return carry

        lax.fori_loop(0, CHUNKS, send, 0)

    def propagate(sweep):
        base = 4 * sweep
        fine_group(base, 0)
        guesses(sweep)
        if sweep == 0:
            @pl.when(bottom)
            def _():
                pl.semaphore_wait(here, 2)
                signal(barrier, (NTS - 1, s))
                pass_class()
                pass_heads(UNITS[:2])
                pass_tails()
                pass_heads(UNITS[2:])

            share_class()
        else:
            pass_planes()
        for d in range(1, HALO + 1):
            wait_halo(sweep, d - 1)
            if sweep == 0 and d >= 2:
                take_class(d - 2)
            fine_group(base, d)
            if d + 1 >= FINE:
                if sweep == 0 and d + 1 == FINE:
                    pl.semaphore_wait(ready, 1)
                low = 2 * HALO - d
                last_step(sweep, low)
                last_step(sweep, DEEP - 1 - low)

    def state_copy(sweep, target, src):
        if sweep == 0:
            dst = lv.at[4, HALO + my_plane, :, :, my_columns]
        else:
            dst = out.at[0, :, my_plane, :, my_columns]
        return (
            pltpu.make_async_remote_copy(
                src_ref=src,
                dst_ref=dst,
                send_sem=vs.at[sweep, target],
                recv_sem=vr.at[sweep, my_plane],
                device_id=(target, s),
                device_id_type=MESH,
            ),
            pltpu.make_async_copy(src, dst, vr.at[sweep, my_plane]),
        )

    def send_state(sweep, target, src):
        there, local = state_copy(sweep, target, src)

        @pl.when(target != t)
        def _():
            there.start()

        @pl.when(target == t)
        def _():
            local.start()

        if sweep == 0:
            send_over(target, src)

    def wait_piece(sweep, j):
        pltpu.make_async_copy(got.at[sweep, j], got.at[sweep, j], pr.at[sweep, j]).wait()

    def unpack(sweep, j):
        edges = got[sweep, j, 2 * ROWS : PIECE]
        parts = [pltpu.roll(edges, LANES - (32 * quarter + 16), 1) for quarter in range(4)]
        fields = []
        for field in range(2):
            side = jnp.concatenate(parts[2 * field : 2 * field + 2], axis=0)
            main = got[sweep, j, field * ROWS : (field + 1) * ROWS]
            fields.append(jnp.concatenate([main, side], axis=1))
        return fields

    def relay(sweep):
        columns = [
            pl.ds(pl.multiple_of(lax.rem(my_chunk + k, CHUNKS) * LANES, LANES), LANES)
            for k in (0, 1, CHUNKS - 1)
        ]
        wide = lax.broadcasted_iota(jnp.int32, (ROWS, LANES), 1)
        maps = []
        for field in range(2):
            here, after, before = [lam[HALO + my_plane, field, :, c] for c in columns]
            both = jnp.concatenate([here, jnp.where(wide < 64, after, before)], axis=1)
            maps.append(coarse_of(both))
        wait_piece(sweep, sweep)
        u, v = unpack(sweep, sweep)
        if sweep == 0:
            made[0, 0, 0] = u[:, :LANES]
            made[0, 0, 1] = v[:, :LANES]
            send_state(0, 1, made.at[0, 0])

        def step(m, carry):
            u, v = carry
            j = m + sweep
            wait_piece(sweep, j)
            cu, cv = unpack(sweep, j)
            u, v = coarse(u, v, maps[0], maps[1])
            u, v = u + cu, v + cv
            made[sweep, m, 0] = u[:, :LANES]
            made[sweep, m, 1] = v[:, :LANES]
            send_state(sweep, m + 1, made.at[sweep, m])
            return u, v

        lax.fori_loop(1, NTS - 1, step, (u, v))

    @pl.when(jnp.logical_not(last))
    def _():
        propagate(0)

    @pl.when(last)
    def _():
        for i in range(HALO - 1):
            take_class(i)

    relay(0)

    def wait_plane(sweep, p):
        if sweep == 0:
            ref = lv.at[4, HALO + p]
        else:
            ref = out.at[0, :, p]
        pltpu.make_async_copy(ref, ref, vr.at[sweep, p]).wait()

    @pl.when(t > 0)
    def _():
        wait_plane(0, PLANES - 1)
        wait_plane(0, 0)
        send_planes((0, 3))
        wait_plane(0, 1)
        wait_plane(0, 2)
        send_planes((1, 2))
        propagate(1)

    relay(1)

    @pl.when(t > 1)
    def _():
        for p in range(PLANES):
            wait_plane(1, p)

    drain_class()

    @pl.when(jnp.logical_not(last))
    def _():
        drain_starts()

    @pl.when(t > 0)
    def _():
        drain_planes()

    for sweep in range(2):
        sender = t < NTS - 1 if sweep == 0 else t > 0

        def drain(owner, carry):
            @pl.when(sender & (owner != t))
            def _():
                piece_copy(sweep, owner).wait_send()

            @pl.when((owner != t) & (owner > sweep))
            def _():
                state_copy(sweep, owner, made.at[sweep, 0])[0].wait_send()

            if sweep == 0:
                @pl.when(end & (owner > 0))
                def _():
                    straight_copy(owner, made.at[0, 0]).wait_send()

            return carry

        lax.fori_loop(0, NTS, drain, 0)


def on_device(slice_starts, class_map, table):
    field, dma = (2, ROWS, COLS), pltpu.SemaphoreType.DMA
    return pl.pallas_call(
        kernel,
        out_shape=jax.ShapeDtypeStruct(slice_starts.shape, jnp.float32),
        in_specs=[
            pl.BlockSpec(memory_space=pl.ANY),
            pl.BlockSpec(memory_space=pl.ANY),
            pl.BlockSpec(memory_space=pltpu.SMEM),
        ],
        out_specs=pl.BlockSpec(memory_space=pltpu.VMEM),
        scratch_shapes=[
            pltpu.VMEM((2 * FINE, DEEP) + field, jnp.float32),
            pltpu.VMEM((DEEP, ROWS, COLS), jnp.int32),
            pltpu.VMEM((DEEP,) + field, jnp.float32),
            pltpu.VMEM((PLANES,) + field, jnp.float32),
            pltpu.VMEM((2, NTS, PIECE, LANES), jnp.float32),
            pltpu.VMEM((2, NTS, PIECE, LANES), jnp.float32),
            pltpu.VMEM((2, NTS, 2, ROWS, LANES), jnp.float32),
            pltpu.VMEM((len(ROUND), ROWS, COLS), jnp.float32),
            pltpu.VMEM((HALO, 2, ROWS, COLS), jnp.float32),
            pltpu.VMEM((HALO - 1, ROWS, COLS), jnp.int32),
            pltpu.VMEM((HALO // 2,) + field, jnp.float32),
            dma((PLANES + 1,)),
            dma((2, HALO, 2)),
            dma((2, HALO, 2)),
            dma((len(ROUND),)),
            dma((len(ROUND),)),
            dma((HALO, 2)),
            dma((HALO, 2)),
            dma((2, HALO - 1)),
            dma((2, HALO - 1)),
            dma((2, HALO - 1)),
            dma((2, HALO - 1)),
            dma((HALO - 1,)),
            dma((HALO - 1,)),
            dma((2, HALO)),
            dma((2, HALO)),
            dma((NTS,)),
            dma((HALO // 2,)),
            dma((HALO // 2,)),
            dma((2, NTS)),
            dma((2, NTS)),
            dma((2, NTS)),
            dma((2, PLANES)),
            pltpu.SemaphoreType.REGULAR,
            pltpu.SemaphoreType.REGULAR,
        ],
        compiler_params=pltpu.CompilerParams(
            collective_id=0, has_side_effects=True, vmem_limit_bytes=60 * 1024 * 1024
        ),
        name="parareal",
    )(slice_starts, class_map, table.T)


def solution(mesh):
    in_specs = (P("tm", None, "slab", None, None), P("slab", None, None), P())
    out_specs = P("tm", None, "slab", None, None)
    return jax.shard_map(
        on_device, mesh=mesh, in_specs=in_specs, out_specs=out_specs, check_vma=False
    )
```

```python
import functools

import jax
import jax.numpy as jnp
from jax import lax
from jax.experimental import pallas as pl
from jax.experimental.pallas import tpu as pltpu
from jax.sharding import PartitionSpec as P

FINE = 4
CLASSES = 4
NTS = 16
FEED = 0.04
KILL = 0.062
STEP = 0.04
PLANES = 4
ROWS = 16
COLS = 512
LANES = 128
CHUNKS = COLS // LANES
HALO = FINE
DEEP = PLANES + 2 * HALO
PIECE = 2 * ROWS + 8
MESH = pl.DeviceIdType.MESH
TALL = 8
ROUND = ((3, 0), (3, 1), (2, 1))
NEAR = 2


def react(u, v, scale):
    uvv = u * v * v
    return scale * (FEED * (1.0 - u) - uvv), scale * (uvv - (FEED + KILL) * v)


def four(a):
    rows, cols = a.shape
    return (
        pltpu.roll(a, 1, 1)
        + pltpu.roll(a, cols - 1, 1)
        + pltpu.roll(a, 1, 0)
        + pltpu.roll(a, rows - 1, 0)
    )


def coarse(u, v, cu, cv):
    ru, rv = react(u, v, FINE * STEP)
    return u + cu * (four(u) - 4.0 * u) + ru, v + cv * (four(v) - 4.0 * v) + rv


def coarse_of(lam):
    return FINE * lam / (1.0 + 4.0 * FINE * lam)


def kernel(
    ss, cm_in, table, out,
    lv, cm, lam, gb, pack, got, made, tails, heads, kinds, planes,
    load_sem, hs, hr, ts, tr, ds, dr, cs, cr, xs, xr, ks, kr,
    gs, gr, es, er, fs, ps, pr, vs, vr, ready, here,
):
    t = lax.axis_index("tm")
    s = lax.axis_index("slab")
    slabs = lax.axis_size("slab")
    up = lax.rem(s + 1, slabs)
    down = lax.rem(s + slabs - 1, slabs)
    my_plane = lax.rem(t, PLANES)
    my_chunk = t // PLANES
    my_columns = pl.ds(pl.multiple_of(my_chunk * LANES, LANES), LANES)
    core = lax.rem(t, 2)
    partner = t + 1 - 2 * core
    last = t == NTS - 1
    height = lax.rem(s, TALL)
    top, bottom = height == TALL - 1, height == 0
    end = top | bottom
    across = jnp.where(top, s - (TALL - 1), jnp.where(bottom, s + (TALL - 1), s))
    beside_up = lax.rem(s + TALL, slabs)
    beside_down = lax.rem(s + slabs - TALL, slabs)
    UP, DOWN = 0, 1

    def signal(sem, where):
        pl.semaphore_signal(sem, inc=1, device_id=where, device_id_type=MESH)

    def remote(src, dst, send, recv, where):
        return pltpu.make_async_remote_copy(
            src_ref=src,
            dst_ref=dst,
            send_sem=send,
            recv_sem=recv,
            device_id=where,
            device_id_type=MESH,
        )

    def arrived(ref, sem):
        pltpu.make_async_copy(ref, ref, sem).wait()

    barrier = pltpu.get_barrier_semaphore()
    signal(barrier, (partner, s))
    signal(barrier, (t, down))

    @pl.when(jnp.logical_not(top))
    def _():
        signal(barrier, (t, up))

    @pl.when(bottom)
    def _():
        for z in (across, beside_up, beside_down):
            signal(barrier, (t, z))

    @pl.when(jnp.logical_not(last | end))
    def _():
        signal(barrier, (NTS - 1, s))

    loads = [
        pltpu.make_async_copy(ss.at[0, :, p], lv.at[0, HALO + p], load_sem.at[p])
        for p in range(PLANES)
    ]
    loads.append(pltpu.make_async_copy(cm_in, cm.at[pl.ds(HALO, PLANES)], load_sem.at[PLANES]))
    for copy in loads:
        copy.start()
    pl.semaphore_wait(barrier, 3 + jnp.where(end, 1, 0) + jnp.where(last, NTS - 1, 0))

    @pl.when(top)
    def _():
        signal(here, (t, up))
        signal(here, (t, across))

        @pl.when(jnp.logical_not(last))
        def _():
            signal(barrier, (NTS - 1, s))

    @pl.when(last)
    def _():
        @pl.when(bottom)
        def _():
            pl.semaphore_wait(here, 2)

        def tell(peer, carry):
            signal(ready, (peer, s))
            return carry

        lax.fori_loop(0, NTS - 1, tell, 0)

    def carrier(way):
        return ((core == way) & (t < NTS - 2)) | (t == NTS - 2)

    def class_planes(way, i):
        return (PLANES - 1 - i, HALO - 1 - i) if way == UP else (i, HALO + PLANES + i)

    def class_copy(way, i):
        src, plane = class_planes(way, i)
        return remote(
            cm_in.at[src], cm.at[plane], cs.at[way, i], cr.at[way, i], (t, down if way else up)
        )

    def kind_copy(i):
        return remote(cm_in.at[i], kinds.at[i], cs.at[DOWN, i], kr.at[i], (t, beside_down))

    def kind_forward(i):
        return remote(
            kinds.at[i], cm.at[HALO + PLANES + i], ks.at[i], cr.at[DOWN, i], (t, across)
        )

    def class_share(way, i):
        plane = class_planes(way, i)[1]
        return remote(cm.at[plane], cm.at[plane], xs.at[way, i], xr.at[way, i], (partner, s))

    def send_class():
        @pl.when(carrier(UP))
        def _():
            for i in range(HALO - 1):
                class_copy(UP, i).start()

        @pl.when(carrier(DOWN) & bottom)
        def _():
            for i in range(HALO - 1):
                kind_copy(i).start()

        @pl.when(carrier(DOWN) & jnp.logical_not(bottom))
        def _():
            for i in range(HALO - 1):
                class_copy(DOWN, i).start()

    def pass_class():
        @pl.when(carrier(DOWN))
        def _():
            for i in range(HALO - 1):
                copy = kind_forward(i)
                kind_copy(i).wait_recv()
                copy.start()

    def share_class():
        for way in (UP, DOWN):

            @pl.when(carrier(way))
            def _():
                for i in range(HALO - 1):
                    share = class_share(way, i)
                    class_copy(way, i).wait_recv()
                    share.start()

    def take_class(i):
        for way in (UP, DOWN):

            @pl.when(jnp.logical_not(carrier(way)))
            def _():
                class_share(way, i).wait_recv()

        diffusivity(HALO - 1 - i)
        diffusivity(HALO + PLANES + i)

    def drain_class():
        for way in (UP, DOWN):

            @pl.when(carrier(way))
            def _():
                for i in range(HALO - 1):
                    class_copy(way, i).wait_send()
                    class_share(way, i).wait_send()

        @pl.when(bottom & carrier(DOWN))
        def _():
            for i in range(HALO - 1):
                kind_forward(i).wait_send()

    def unit_source(way, i, field):
        return ss.at[0, field, PLANES - 1 - i if way == UP else i]

    def unit_target(way, i, field):
        return lv.at[0, HALO - 1 - i if way == UP else HALO + PLANES + i, field]

    def unit_copy(way, i, field):
        return remote(
            unit_source(way, i, field),
            unit_target(way, i, field),
            hs.at[way, i, field],
            hr.at[way, i, field],
            (t, up if way == UP else down),
        )

    def tail_copy(n):
        i, field = ROUND[n]
        return remote(
            unit_source(UP, i, field), tails.at[n], hs.at[UP, i, field], tr.at[n], (t, across)
        )

    def tail_forward(n):
        i, field = ROUND[n]
        return remote(
            tails.at[n], unit_target(UP, i, field), ts.at[n], hr.at[UP, i, field], (t, beside_up)
        )

    def head_copy(i, field):
        return remote(
            unit_source(DOWN, i, field),
            heads.at[i, field],
            hs.at[DOWN, i, field],
            dr.at[i, field],
            (t, beside_down),
        )

    def head_forward(i, field):
        return remote(
            heads.at[i, field],
            unit_target(DOWN, i, field),
            ds.at[i, field],
            hr.at[DOWN, i, field],
            (t, across),
        )

    UNITS = [(i, field) for i in range(HALO) for field in range(2)]

    def send_starts():
        @pl.when(top)
        def _():
            for i, field in UNITS[:2]:
                unit_copy(UP, i, field).start()
            for n in range(len(ROUND)):
                tail_copy(n).start()
            for i, field in UNITS[2:]:
                if (i, field) not in ROUND:
                    unit_copy(UP, i, field).start()
            for i, field in UNITS:
                unit_copy(DOWN, i, field).start()

        @pl.when(bottom)
        def _():
            for i, field in UNITS:
                head_copy(i, field).start()
                unit_copy(UP, i, field).start()

        @pl.when(jnp.logical_not(end))
        def _():
            for i, field in UNITS:
                unit_copy(UP, i, field).start()
                unit_copy(DOWN, i, field).start()

    def pass_heads(units):
        for i, field in units:
            copy = head_forward(i, field)
            head_copy(i, field).wait_recv()
            copy.start()

    def pass_tails():
        for n in range(len(ROUND)):
            copy = tail_forward(n)
            tail_copy(n).wait_recv()
            copy.start()

    def drain_starts():
        for way in (UP, DOWN):
            for i, field in UNITS:
                unit_copy(way, i, field).wait_send()

        @pl.when(bottom)
        def _():
            for i, field in UNITS:
                head_forward(i, field).wait_send()
            for n in range(len(ROUND)):
                tail_forward(n).wait_send()

    def outer(way, i):
        return lv.at[4, HALO - 1 - i if way == UP else HALO + PLANES + i]

    def plane_copy(way, i):
        return remote(
            lv.at[4, HALO + (PLANES - 1 - i if way == UP else i)],
            outer(way, i),
            gs.at[way, i],
            gr.at[way, i],
            (t, up if way == UP else down),
        )

    def send_planes(each):
        for way, over in ((UP, top), (DOWN, bottom)):

            @pl.when(jnp.logical_not(over))
            def _():
                for i in each:
                    plane_copy(way, i).start()

    def plane_forward(i):
        n = i - NEAR
        return remote(
            planes.at[n],
            lv.at[4, jnp.where(bottom, HALO - 1 - i, HALO + PLANES + i)],
            fs.at[n],
            gr.at[jnp.where(bottom, UP, DOWN), i],
            (t, jnp.where(bottom, beside_up, beside_down)),
        )

    def pass_planes():
        @pl.when(end)
        def _():
            for i in range(NEAR, HALO):
                n = i - NEAR
                copy = plane_forward(i)
                arrived(planes.at[n], er.at[n])
                copy.start()

    def drain_planes():
        for way, over in ((UP, top), (DOWN, bottom)):

            @pl.when(jnp.logical_not(over))
            def _():
                for i in range(HALO):
                    plane_copy(way, i).wait_send()

        @pl.when(end)
        def _():
            for i in range(NEAR, HALO):
                plane_forward(i).wait_send()

    far = jnp.where(top, PLANES - 1 - my_plane, my_plane)

    def straight_copy(target, src):
        return remote(
            src,
            lv.at[4, jnp.where(top, my_plane, HALO + PLANES + my_plane), :, :, my_columns],
            es.at[target],
            gr.at[jnp.where(top, UP, DOWN), far],
            (target, jnp.where(top, up, down)),
        )

    def round_copy(target, src):
        n = jnp.where(far < NEAR, 0, far - NEAR)
        return remote(
            src, planes.at[n, :, :, my_columns], es.at[target], er.at[n], (target, across)
        )

    def send_over(target, src):
        @pl.when(end & (far < NEAR))
        def _():
            straight_copy(target, src).start()

        @pl.when(end & (far >= NEAR))
        def _():
            round_copy(target, src).start()

    def wait_halo(sweep, i):
        for way in (UP, DOWN):
            if sweep == 0:
                for field in range(2):
                    unit_copy(way, i, field).wait_recv()
            else:
                arrived(outer(way, i), gr.at[way, i])

    send_class()

    @pl.when(jnp.logical_not(last))
    def _():
        send_starts()

    def diffusivity(plane):
        klass = cm[plane]
        for field in range(2):
            value = jnp.zeros(klass.shape, jnp.float32)
            for k in range(CLASSES):
                value = jnp.where(klass == k, table[field, k], value)
            lam[plane, field] = value

    for copy in loads:
        copy.wait()

    def own_lam(p, carry):
        diffusivity(HALO + p)
        return carry

    lax.fori_loop(0, PLANES, own_lam, 0)

    def fine(base, level, plane):
        u, v = lv[base + level - 1, plane, 0], lv[base + level - 1, plane, 1]
        lap_u = lv[base + level - 1, plane - 1, 0] + lv[base + level - 1, plane + 1, 0]
        lap_v = lv[base + level - 1, plane - 1, 1] + lv[base + level - 1, plane + 1, 1]
        lap_u = lap_u + four(u) - 6.0 * u
        lap_v = lap_v + four(v) - 6.0 * v
        ru, rv = react(u, v, STEP)
        return u + lam[plane, 0] * lap_u + ru, v + lam[plane, 1] * lap_v + rv

    def fine_group(base, d):
        def step(k, carry):
            low = HALO - d + k
            for plane in (low, DEEP - 1 - low):
                u, v = fine(base, k, plane)
                lv[base + k, plane, 0] = u
                lv[base + k, plane, 1] = v
            return carry

        lax.fori_loop(1, min(d + 1, FINE - 1) + 1, step, 0)

    def guesses(sweep):
        keep = jnp.where(t == sweep, 0.0, 1.0).astype(jnp.float32)

        def one(p, carry):
            q = HALO + p
            cu, cv = coarse_of(lam[q, 0]), coarse_of(lam[q, 1])
            gu, gv = coarse(lv[4 * sweep, q, 0], lv[4 * sweep, q, 1], cu, cv)
            gb[p, 0] = keep * gu
            gb[p, 1] = keep * gv
            return carry

        lax.fori_loop(0, PLANES, one, 0)

    def piece_copy(sweep, owner):
        return pltpu.make_async_remote_copy(
            src_ref=pack.at[sweep, owner],
            dst_ref=got.at[sweep, t],
            send_sem=ps.at[sweep, owner],
            recv_sem=pr.at[sweep, t],
            device_id=(owner, s),
            device_id_type=MESH,
        )

    lane = lax.broadcasted_iota(jnp.int32, (8, LANES), 1)

    def last_step(sweep, q):
        p = q - HALO
        u, v = fine(4 * sweep, FINE, q)
        @pl.when(t == sweep)
        def _():
            out[0, 0, p] = u
            out[0, 1, p] = v
        u = u - gb[p, 0]
        v = v - gb[p, 1]
        for c in range(CHUNKS):
            owner = c * PLANES + p
            here = slice(c * LANES, (c + 1) * LANES)
            after = ((c + 1) % CHUNKS) * LANES
            before = ((c - 1) % CHUNKS) * LANES
            pack[sweep, owner, 0:ROWS] = u[:, here]
            pack[sweep, owner, ROWS : 2 * ROWS] = v[:, here]
            edges = None
            for quarter, (field, row) in enumerate(((u, 0), (u, 8), (v, 0), (v, 8))):
                both = jnp.where(
                    lane < 64,
                    field[row : row + 8, after : after + LANES],
                    field[row : row + 8, before : before + LANES],
                )
                both = pltpu.roll(both, 32 * quarter + 16, 1)
                edges = both if edges is None else jnp.where(lane // 32 == quarter, both, edges)
            pack[sweep, owner, 2 * ROWS : PIECE] = edges

        def send(c, carry):
            owner = c * PLANES + p

            @pl.when(owner != t)
            def _():
                piece_copy(sweep, owner).start()

            @pl.when(owner == t)
            def _():
                pltpu.make_async_copy(
                    pack.at[sweep, owner], got.at[sweep, t], pr.at[sweep, t]
                ).start()

            return carry

        lax.fori_loop(0, CHUNKS, send, 0)

    def propagate(sweep):
        base = 4 * sweep
        fine_group(base, 0)
        guesses(sweep)
        if sweep == 0:
            @pl.when(bottom)
            def _():
                pl.semaphore_wait(here, 2)
                signal(barrier, (NTS - 1, s))
                pass_class()
                pass_heads(UNITS[:2])
                pass_tails()
                pass_heads(UNITS[2:])

            share_class()
        else:
            pass_planes()
        for d in range(1, HALO + 1):
            wait_halo(sweep, d - 1)
            if sweep == 0 and d >= 2:
                take_class(d - 2)
            fine_group(base, d)
            if d + 1 >= FINE:
                if sweep == 0 and d + 1 == FINE:
                    pl.semaphore_wait(ready, 1)
                low = 2 * HALO - d
                last_step(sweep, low)
                last_step(sweep, DEEP - 1 - low)

    def state_copy(sweep, target, src):
        if sweep == 0:
            dst = lv.at[4, HALO + my_plane, :, :, my_columns]
        else:
            dst = out.at[0, :, my_plane, :, my_columns]
        return (
            pltpu.make_async_remote_copy(
                src_ref=src,
                dst_ref=dst,
                send_sem=vs.at[sweep, target],
                recv_sem=vr.at[sweep, my_plane],
                device_id=(target, s),
                device_id_type=MESH,
            ),
            pltpu.make_async_copy(src, dst, vr.at[sweep, my_plane]),
        )

    def send_state(sweep, target, src):
        there, local = state_copy(sweep, target, src)

        @pl.when(target != t)
        def _():
            there.start()

        @pl.when(target == t)
        def _():
            local.start()


    def wait_piece(sweep, j):
        pltpu.make_async_copy(got.at[sweep, j], got.at[sweep, j], pr.at[sweep, j]).wait()

    def unpack(sweep, j):
        edges = got[sweep, j, 2 * ROWS : PIECE]
        parts = [pltpu.roll(edges, LANES - (32 * quarter + 16), 1) for quarter in range(4)]
        fields = []
        for field in range(2):
            side = jnp.concatenate(parts[2 * field : 2 * field + 2], axis=0)
            main = got[sweep, j, field * ROWS : (field + 1) * ROWS]
            fields.append(jnp.concatenate([main, side], axis=1))
        return fields

    def relay(sweep):
        columns = [
            pl.ds(pl.multiple_of(lax.rem(my_chunk + k, CHUNKS) * LANES, LANES), LANES)
            for k in (0, 1, CHUNKS - 1)
        ]
        wide = lax.broadcasted_iota(jnp.int32, (ROWS, LANES), 1)
        maps = []
        for field in range(2):
            here, after, before = [lam[HALO + my_plane, field, :, c] for c in columns]
            both = jnp.concatenate([here, jnp.where(wide < 64, after, before)], axis=1)
            maps.append(coarse_of(both))
        wait_piece(sweep, sweep)
        u, v = unpack(sweep, sweep)
        if sweep == 0:
            made[0, 0, 0] = u[:, :LANES]
            made[0, 0, 1] = v[:, :LANES]
            send_state(0, 1, made.at[0, 0])

        def step(m, carry):
            u, v = carry
            j = m + sweep
            wait_piece(sweep, j)
            cu, cv = unpack(sweep, j)
            u, v = coarse(u, v, maps[0], maps[1])
            u, v = u + cu, v + cv
            made[sweep, m, 0] = u[:, :LANES]
            made[sweep, m, 1] = v[:, :LANES]
            send_state(sweep, m + 1, made.at[sweep, m])
            return u, v

        lax.fori_loop(1, NTS - 1, step, (u, v))
        if sweep == 0:
            def over(k, carry):
                send_over(k + 1, made.at[0, k])
                return carry

            lax.fori_loop(0, NTS - 1, over, 0)

    @pl.when(jnp.logical_not(last))
    def _():
        propagate(0)

    @pl.when(last)
    def _():
        for i in range(HALO - 1):
            take_class(i)

    relay(0)

    def wait_plane(sweep, p):
        if sweep == 0:
            ref = lv.at[4, HALO + p]
        else:
            ref = out.at[0, :, p]
        pltpu.make_async_copy(ref, ref, vr.at[sweep, p]).wait()

    @pl.when(t > 0)
    def _():
        wait_plane(0, PLANES - 1)
        wait_plane(0, 0)
        send_planes((0, 3))
        wait_plane(0, 1)
        wait_plane(0, 2)
        send_planes((1, 2))
        propagate(1)

    relay(1)

    @pl.when(t > 1)
    def _():
        for p in range(PLANES):
            wait_plane(1, p)

    drain_class()

    @pl.when(jnp.logical_not(last))
    def _():
        drain_starts()

    @pl.when(t > 0)
    def _():
        drain_planes()

    for sweep in range(2):
        sender = t < NTS - 1 if sweep == 0 else t > 0

        def drain(owner, carry):
            @pl.when(sender & (owner != t))
            def _():
                piece_copy(sweep, owner).wait_send()

            @pl.when((owner != t) & (owner > sweep))
            def _():
                state_copy(sweep, owner, made.at[sweep, 0])[0].wait_send()

            if sweep == 0:
                @pl.when(end & (owner > 0))
                def _():
                    straight_copy(owner, made.at[0, 0]).wait_send()

            return carry

        lax.fori_loop(0, NTS, drain, 0)


def on_device(slice_starts, class_map, table):
    field, dma = (2, ROWS, COLS), pltpu.SemaphoreType.DMA
    return pl.pallas_call(
        kernel,
        out_shape=pltpu.VMEM(slice_starts.shape, jnp.float32),
        in_specs=[
            pl.BlockSpec(memory_space=pl.ANY),
            pl.BlockSpec(memory_space=pl.ANY),
            pl.BlockSpec(memory_space=pltpu.SMEM),
        ],
        out_specs=pl.BlockSpec(memory_space=pltpu.VMEM),
        scratch_shapes=[
            pltpu.VMEM((2 * FINE, DEEP) + field, jnp.float32),
            pltpu.VMEM((DEEP, ROWS, COLS), jnp.int32),
            pltpu.VMEM((DEEP,) + field, jnp.float32),
            pltpu.VMEM((PLANES,) + field, jnp.float32),
            pltpu.VMEM((2, NTS, PIECE, LANES), jnp.float32),
            pltpu.VMEM((2, NTS, PIECE, LANES), jnp.float32),
            pltpu.VMEM((2, NTS, 2, ROWS, LANES), jnp.float32),
            pltpu.VMEM((len(ROUND), ROWS, COLS), jnp.float32),
            pltpu.VMEM((HALO, 2, ROWS, COLS), jnp.float32),
            pltpu.VMEM((HALO - 1, ROWS, COLS), jnp.int32),
            pltpu.VMEM((HALO - NEAR,) + field, jnp.float32),
            dma((PLANES + 1,)),
            dma((2, HALO, 2)),
            dma((2, HALO, 2)),
            dma((len(ROUND),)),
            dma((len(ROUND),)),
            dma((HALO, 2)),
            dma((HALO, 2)),
            dma((2, HALO - 1)),
            dma((2, HALO - 1)),
            dma((2, HALO - 1)),
            dma((2, HALO - 1)),
            dma((HALO - 1,)),
            dma((HALO - 1,)),
            dma((2, HALO)),
            dma((2, HALO)),
            dma((NTS,)),
            dma((HALO - NEAR,)),
            dma((HALO - NEAR,)),
            dma((2, NTS)),
            dma((2, NTS)),
            dma((2, NTS)),
            dma((2, PLANES)),
            pltpu.SemaphoreType.REGULAR,
            pltpu.SemaphoreType.REGULAR,
        ],
        compiler_params=pltpu.CompilerParams(
            collective_id=0, has_side_effects=True, vmem_limit_bytes=60 * 1024 * 1024
        ),
        name="parareal",
    )(slice_starts, class_map, table.T)


def solution(mesh):
    in_specs = (P("tm", None, "slab", None, None), P("slab", None, None), P())
    out_specs = P("tm", None, "slab", None, None)
    return jax.shard_map(
        on_device, mesh=mesh, in_specs=in_specs, out_specs=out_specs, check_vma=False
    )
```

```python
import functools

import jax
import jax.numpy as jnp
from jax import lax
from jax.experimental import pallas as pl
from jax.experimental.pallas import tpu as pltpu
from jax.sharding import PartitionSpec as P

FINE = 4
CLASSES = 4
NTS = 16
FEED = 0.04
KILL = 0.062
STEP = 0.04
PLANES = 4
ROWS = 16
COLS = 512
LANES = 128
CHUNKS = COLS // LANES
HALO = FINE
DEEP = PLANES + 2 * HALO
PIECE = 2 * ROWS + 8
MESH = pl.DeviceIdType.MESH
TALL = 8
ROUND = ((3, 0), (3, 1), (2, 1))
NEAR = 2
LATE = ((3, 0), (3, 1))


def react(u, v, scale):
    uvv = u * v * v
    return scale * (FEED * (1.0 - u) - uvv), scale * (uvv - (FEED + KILL) * v)


def four(a):
    rows, cols = a.shape
    return (
        pltpu.roll(a, 1, 1)
        + pltpu.roll(a, cols - 1, 1)
        + pltpu.roll(a, 1, 0)
        + pltpu.roll(a, rows - 1, 0)
    )


def coarse(u, v, cu, cv):
    ru, rv = react(u, v, FINE * STEP)
    return u + cu * (four(u) - 4.0 * u) + ru, v + cv * (four(v) - 4.0 * v) + rv


def coarse_of(lam):
    return FINE * lam / (1.0 + 4.0 * FINE * lam)


def kernel(
    ss, cm_in, table, out,
    lv, cm, lam, gb, pack, got, made, tails, heads, late, kinds, planes,
    load_sem, hs, hr, ts, tr, ls, lr, ds, dr, cs, cr, xs, xr, ks, kr,
    gs, gr, es, er, fs, ps, pr, vs, vr, ready, here,
):
    t = lax.axis_index("tm")
    s = lax.axis_index("slab")
    slabs = lax.axis_size("slab")
    up = lax.rem(s + 1, slabs)
    down = lax.rem(s + slabs - 1, slabs)
    my_plane = lax.rem(t, PLANES)
    my_chunk = t // PLANES
    my_columns = pl.ds(pl.multiple_of(my_chunk * LANES, LANES), LANES)
    core = lax.rem(t, 2)
    partner = t + 1 - 2 * core
    last = t == NTS - 1
    height = lax.rem(s, TALL)
    top, bottom = height == TALL - 1, height == 0
    end = top | bottom
    across = jnp.where(top, s - (TALL - 1), jnp.where(bottom, s + (TALL - 1), s))
    beside_up = lax.rem(s + TALL, slabs)
    beside_down = lax.rem(s + slabs - TALL, slabs)
    UP, DOWN = 0, 1

    def signal(sem, where):
        pl.semaphore_signal(sem, inc=1, device_id=where, device_id_type=MESH)

    def remote(src, dst, send, recv, where):
        return pltpu.make_async_remote_copy(
            src_ref=src,
            dst_ref=dst,
            send_sem=send,
            recv_sem=recv,
            device_id=where,
            device_id_type=MESH,
        )

    def arrived(ref, sem):
        pltpu.make_async_copy(ref, ref, sem).wait()

    barrier = pltpu.get_barrier_semaphore()
    signal(barrier, (partner, s))
    signal(barrier, (t, down))

    @pl.when(jnp.logical_not(top))
    def _():
        signal(barrier, (t, up))

    @pl.when(bottom)
    def _():
        for z in (across, beside_up, beside_down):
            signal(barrier, (t, z))

    @pl.when(jnp.logical_not(last | end))
    def _():
        signal(barrier, (NTS - 1, s))

    loads = [
        pltpu.make_async_copy(ss.at[0, :, p], lv.at[0, HALO + p], load_sem.at[p])
        for p in range(PLANES)
    ]
    loads.append(pltpu.make_async_copy(cm_in, cm.at[pl.ds(HALO, PLANES)], load_sem.at[PLANES]))
    for copy in loads:
        copy.start()
    pl.semaphore_wait(barrier, 3 + jnp.where(end, 1, 0) + jnp.where(last, NTS - 1, 0))

    @pl.when(top)
    def _():
        signal(here, (t, up))
        signal(here, (t, across))

        @pl.when(jnp.logical_not(last))
        def _():
            signal(barrier, (NTS - 1, s))

    @pl.when(last)
    def _():
        @pl.when(bottom)
        def _():
            pl.semaphore_wait(here, 2)

        def tell(peer, carry):
            signal(ready, (peer, s))
            return carry

        lax.fori_loop(0, NTS - 1, tell, 0)

    def carrier(way):
        return ((core == way) & (t < NTS - 2)) | (t == NTS - 2)

    def class_planes(way, i):
        return (PLANES - 1 - i, HALO - 1 - i) if way == UP else (i, HALO + PLANES + i)

    def class_copy(way, i):
        src, plane = class_planes(way, i)
        return remote(
            cm_in.at[src], cm.at[plane], cs.at[way], cr.at[way, i], (t, down if way else up)
        )

    def kind_copy(i):
        return remote(cm_in.at[i], kinds.at[i], cs.at[DOWN], kr.at[i], (t, beside_down))

    def kind_forward(i):
        return remote(
            kinds.at[i], cm.at[HALO + PLANES + i], ks, cr.at[DOWN, i], (t, across)
        )

    def class_share(way, i):
        plane = class_planes(way, i)[1]
        return remote(cm.at[plane], cm.at[plane], xs.at[way], xr.at[way, i], (partner, s))

    def send_class():
        @pl.when(carrier(UP))
        def _():
            for i in range(HALO - 1):
                class_copy(UP, i).start()

        @pl.when(carrier(DOWN) & bottom)
        def _():
            for i in range(HALO - 1):
                kind_copy(i).start()

        @pl.when(carrier(DOWN) & jnp.logical_not(bottom))
        def _():
            for i in range(HALO - 1):
                class_copy(DOWN, i).start()

    def pass_class():
        @pl.when(carrier(DOWN))
        def _():
            for i in range(HALO - 1):
                copy = kind_forward(i)
                kind_copy(i).wait_recv()
                copy.start()

    def share_class():
        for way in (UP, DOWN):

            @pl.when(carrier(way))
            def _():
                for i in range(HALO - 1):
                    share = class_share(way, i)
                    class_copy(way, i).wait_recv()
                    share.start()

    def take_class(i):
        for way in (UP, DOWN):

            @pl.when(jnp.logical_not(carrier(way)))
            def _():
                class_share(way, i).wait_recv()

        diffusivity(HALO - 1 - i)
        diffusivity(HALO + PLANES + i)

    def drain_class():
        some = cm.at[pl.ds(0, HALO - 1)]
        for way in (UP, DOWN):

            @pl.when(carrier(way))
            def _():
                arrived(some, cs.at[way])
                arrived(some, xs.at[way])

        @pl.when(bottom & carrier(DOWN))
        def _():
            arrived(kinds, ks)

    def unit_source(way, i, field):
        return ss.at[0, field, PLANES - 1 - i if way == UP else i]

    def unit_target(way, i, field):
        return lv.at[0, HALO - 1 - i if way == UP else HALO + PLANES + i, field]

    def unit_copy(way, i, field):
        return remote(
            unit_source(way, i, field),
            unit_target(way, i, field),
            hs.at[way],
            hr.at[way, i, field],
            (t, up if way == UP else down),
        )

    def tail_copy(n):
        i, field = ROUND[n]
        return remote(
            unit_source(UP, i, field), tails.at[n], hs.at[UP], tr.at[n], (t, across)
        )

    def tail_forward(n):
        i, field = ROUND[n]
        return remote(
            tails.at[n], unit_target(UP, i, field), ts, hr.at[UP, i, field], (t, beside_up)
        )

    def head_copy(i, field):
        return remote(
            unit_source(DOWN, i, field),
            heads.at[i, field],
            hs.at[DOWN],
            dr.at[i, field],
            (t, beside_down),
        )

    def head_forward(i, field):
        return remote(
            heads.at[i, field],
            unit_target(DOWN, i, field),
            ds,
            hr.at[DOWN, i, field],
            (t, across),
        )

    def late_copy(n):
        i, field = LATE[n]
        return remote(
            unit_source(DOWN, i, field), late.at[n], hs.at[DOWN], lr.at[n], (t, across)
        )

    def late_forward(n):
        i, field = LATE[n]
        return remote(
            late.at[n],
            unit_target(DOWN, i, field),
            ls,
            hr.at[DOWN, i, field],
            (t, beside_down),
        )

    UNITS = [(i, field) for i in range(HALO) for field in range(2)]
    EARLY = [unit for unit in UNITS if unit not in LATE]

    def send_starts():
        @pl.when(top)
        def _():
            for i, field in UNITS[:2]:
                unit_copy(UP, i, field).start()
            for n in range(len(ROUND)):
                tail_copy(n).start()
            for i, field in UNITS[2:]:
                if (i, field) not in ROUND:
                    unit_copy(UP, i, field).start()
            for i, field in UNITS:
                unit_copy(DOWN, i, field).start()

        @pl.when(bottom)
        def _():
            for i, field in UNITS:
                if (i, field) in EARLY:
                    head_copy(i, field).start()
                unit_copy(UP, i, field).start()

        @pl.when(jnp.logical_not(end))
        def _():
            for i, field in UNITS:
                unit_copy(UP, i, field).start()
                unit_copy(DOWN, i, field).start()

    def pass_heads(units):
        for i, field in units:
            copy = head_forward(i, field)
            head_copy(i, field).wait_recv()
            copy.start()

    def pass_tails():
        for n in range(len(ROUND)):
            copy = tail_forward(n)
            tail_copy(n).wait_recv()
            copy.start()

    def pass_late():
        for n in range(len(LATE)):
            copy = late_forward(n)
            late_copy(n).wait_recv()
            copy.start()

    def drain_starts():
        for way in (UP, DOWN):
            arrived(lv.at[0, pl.ds(0, HALO)], hs.at[way])

        @pl.when(bottom)
        def _():
            arrived(heads.at[pl.ds(0, len(EARLY) // 2)], ds)
            arrived(tails, ts)

        @pl.when(top)
        def _():
            arrived(late, ls)

    def outer(way, i):
        return lv.at[4, HALO - 1 - i if way == UP else HALO + PLANES + i]

    def plane_copy(way, i):
        return remote(
            lv.at[4, HALO + (PLANES - 1 - i if way == UP else i)],
            outer(way, i),
            gs.at[way],
            gr.at[way, i],
            (t, up if way == UP else down),
        )

    def send_planes(each):
        for way, over in ((UP, top), (DOWN, bottom)):

            @pl.when(jnp.logical_not(over))
            def _():
                for i in each:
                    plane_copy(way, i).start()

    def plane_forward(i):
        n = i - NEAR
        return remote(
            planes.at[n],
            lv.at[4, jnp.where(bottom, HALO - 1 - i, HALO + PLANES + i)],
            fs,
            gr.at[jnp.where(bottom, UP, DOWN), i],
            (t, jnp.where(bottom, beside_up, beside_down)),
        )

    def pass_planes():
        @pl.when(end)
        def _():
            for i in range(NEAR, HALO):
                n = i - NEAR
                copy = plane_forward(i)
                arrived(planes.at[n], er.at[n])
                copy.start()

    def drain_planes():
        for way, over in ((UP, top), (DOWN, bottom)):

            @pl.when(jnp.logical_not(over))
            def _():
                arrived(lv.at[4, pl.ds(0, HALO)], gs.at[way])

        @pl.when(end)
        def _():
            arrived(planes, fs)

    far = jnp.where(top, PLANES - 1 - my_plane, my_plane)

    def straight_copy(target, src):
        return remote(
            src,
            lv.at[4, jnp.where(top, my_plane, HALO + PLANES + my_plane), :, :, my_columns],
            es,
            gr.at[jnp.where(top, UP, DOWN), far],
            (target, jnp.where(top, up, down)),
        )

    def round_copy(target, src):
        n = jnp.where(far < NEAR, 0, far - NEAR)
        return remote(
            src, planes.at[n, :, :, my_columns], es, er.at[n], (target, across)
        )

    def send_over(target, src):
        @pl.when(end & (far < NEAR))
        def _():
            straight_copy(target, src).start()

        @pl.when(end & (far >= NEAR))
        def _():
            round_copy(target, src).start()

    def wait_halo(sweep, i):
        for way in (UP, DOWN):
            if sweep == 0:
                for field in range(2):
                    unit_copy(way, i, field).wait_recv()
            else:
                arrived(outer(way, i), gr.at[way, i])

    send_class()

    @pl.when(jnp.logical_not(last))
    def _():
        send_starts()

    def diffusivity(plane):
        klass = cm[plane]
        for field in range(2):
            value = jnp.zeros(klass.shape, jnp.float32)
            for k in range(CLASSES):
                value = jnp.where(klass == k, table[field, k], value)
            lam[plane, field] = value

    for copy in loads:
        copy.wait()

    def own_lam(p, carry):
        diffusivity(HALO + p)
        return carry

    lax.fori_loop(0, PLANES, own_lam, 0)

    def fine(base, level, plane):
        u, v = lv[base + level - 1, plane, 0], lv[base + level - 1, plane, 1]
        lap_u = lv[base + level - 1, plane - 1, 0] + lv[base + level - 1, plane + 1, 0]
        lap_v = lv[base + level - 1, plane - 1, 1] + lv[base + level - 1, plane + 1, 1]
        lap_u = lap_u + four(u) - 6.0 * u
        lap_v = lap_v + four(v) - 6.0 * v
        ru, rv = react(u, v, STEP)
        return u + lam[plane, 0] * lap_u + ru, v + lam[plane, 1] * lap_v + rv

    def fine_group(base, d):
        def step(k, carry):
            low = HALO - d + k
            for plane in (low, DEEP - 1 - low):
                u, v = fine(base, k, plane)
                lv[base + k, plane, 0] = u
                lv[base + k, plane, 1] = v
            return carry

        lax.fori_loop(1, min(d + 1, FINE - 1) + 1, step, 0)

    def guesses(sweep):
        keep = jnp.where(t == sweep, 0.0, 1.0).astype(jnp.float32)

        def one(p, carry):
            q = HALO + p
            cu, cv = coarse_of(lam[q, 0]), coarse_of(lam[q, 1])
            gu, gv = coarse(lv[4 * sweep, q, 0], lv[4 * sweep, q, 1], cu, cv)
            gb[p, 0] = keep * gu
            gb[p, 1] = keep * gv
            return carry

        lax.fori_loop(0, PLANES, one, 0)

    def piece_copy(sweep, owner):
        return pltpu.make_async_remote_copy(
            src_ref=pack.at[sweep, owner],
            dst_ref=got.at[sweep, t],
            send_sem=ps.at[sweep],
            recv_sem=pr.at[sweep, t],
            device_id=(owner, s),
            device_id_type=MESH,
        )

    lane = lax.broadcasted_iota(jnp.int32, (8, LANES), 1)

    def last_step(sweep, q):
        p = q - HALO
        u, v = fine(4 * sweep, FINE, q)
        @pl.when(t == sweep)
        def _():
            out[0, 0, p] = u
            out[0, 1, p] = v
        u = u - gb[p, 0]
        v = v - gb[p, 1]
        for c in range(CHUNKS):
            owner = c * PLANES + p
            here = slice(c * LANES, (c + 1) * LANES)
            after = ((c + 1) % CHUNKS) * LANES
            before = ((c - 1) % CHUNKS) * LANES
            pack[sweep, owner, 0:ROWS] = u[:, here]
            pack[sweep, owner, ROWS : 2 * ROWS] = v[:, here]
            edges = None
            for quarter, (field, row) in enumerate(((u, 0), (u, 8), (v, 0), (v, 8))):
                both = jnp.where(
                    lane < 64,
                    field[row : row + 8, after : after + LANES],
                    field[row : row + 8, before : before + LANES],
                )
                both = pltpu.roll(both, 32 * quarter + 16, 1)
                edges = both if edges is None else jnp.where(lane // 32 == quarter, both, edges)
            pack[sweep, owner, 2 * ROWS : PIECE] = edges

        def send(k, carry):
            owner = lax.rem(my_chunk + CHUNKS + 2 - k, CHUNKS) * PLANES + p

            @pl.when(owner != t)
            def _():
                piece_copy(sweep, owner).start()

            @pl.when(owner == t)
            def _():
                pltpu.make_async_copy(
                    pack.at[sweep, owner], got.at[sweep, t], pr.at[sweep, t]
                ).start()

            return carry

        lax.fori_loop(0, CHUNKS, send, 0)

    def propagate(sweep):
        base = 4 * sweep
        if sweep == 1:
            pass_planes()
        fine_group(base, 0)
        guesses(sweep)
        if sweep == 0:
            @pl.when(bottom)
            def _():
                pl.semaphore_wait(here, 2)
                signal(barrier, (NTS - 1, s))
                for n in range(len(LATE)):
                    late_copy(n).start()
                pass_class()
                pass_heads(EARLY[:2])
                pass_tails()
                pass_heads(EARLY[2:])

            share_class()

            @pl.when(top)
            def _():
                pass_late()

        if sweep == 1:
            drain_first()
        for d in range(1, HALO + 1):
            wait_halo(sweep, d - 1)
            if sweep == 0 and d >= 2:
                take_class(d - 2)
            fine_group(base, d)
            if d + 1 >= FINE:
                if sweep == 0 and d + 1 == FINE:
                    pl.semaphore_wait(ready, 1)
                low = 2 * HALO - d
                last_step(sweep, low)
                last_step(sweep, DEEP - 1 - low)

    def state_copy(sweep, target, src):
        if sweep == 0:
            dst = lv.at[4, HALO + my_plane, :, :, my_columns]
        else:
            dst = out.at[0, :, my_plane, :, my_columns]
        return (
            pltpu.make_async_remote_copy(
                src_ref=src,
                dst_ref=dst,
                send_sem=vs.at[sweep],
                recv_sem=vr.at[sweep, my_plane],
                device_id=(target, s),
                device_id_type=MESH,
            ),
            pltpu.make_async_copy(src, dst, vr.at[sweep, my_plane]),
        )

    def send_state(sweep, target, src):
        there, local = state_copy(sweep, target, src)

        @pl.when(target != t)
        def _():
            there.start()

        @pl.when(target == t)
        def _():
            local.start()


    def drain_pieces(sweep):
        arrived(pack.at[sweep, pl.ds(0, NTS - 1)], ps.at[sweep])

    def drain_states(sweep):
        for own in (0, 1):

            @pl.when((t > sweep) == bool(own))
            def _():
                arrived(made.at[sweep, pl.ds(0, NTS - 1 - sweep - own)], vs.at[sweep])

    def drain_first():
        drain_class()

        @pl.when(jnp.logical_not(last))
        def _():
            drain_starts()
            drain_pieces(0)

        drain_states(0)

    def wait_piece(sweep, j):
        pltpu.make_async_copy(got.at[sweep, j], got.at[sweep, j], pr.at[sweep, j]).wait()

    def unpack(sweep, j):
        edges = got[sweep, j, 2 * ROWS : PIECE]
        parts = [pltpu.roll(edges, LANES - (32 * quarter + 16), 1) for quarter in range(4)]
        fields = []
        for field in range(2):
            side = jnp.concatenate(parts[2 * field : 2 * field + 2], axis=0)
            main = got[sweep, j, field * ROWS : (field + 1) * ROWS]
            fields.append(jnp.concatenate([main, side], axis=1))
        return fields

    def relay(sweep):
        columns = [
            pl.ds(pl.multiple_of(lax.rem(my_chunk + k, CHUNKS) * LANES, LANES), LANES)
            for k in (0, 1, CHUNKS - 1)
        ]
        wide = lax.broadcasted_iota(jnp.int32, (ROWS, LANES), 1)
        maps = []
        for field in range(2):
            here, after, before = [lam[HALO + my_plane, field, :, c] for c in columns]
            both = jnp.concatenate([here, jnp.where(wide < 64, after, before)], axis=1)
            maps.append(coarse_of(both))
        wait_piece(sweep, sweep)
        u, v = unpack(sweep, sweep)
        if sweep == 0:
            made[0, 0, 0] = u[:, :LANES]
            made[0, 0, 1] = v[:, :LANES]
            send_state(0, 1, made.at[0, 0])

        def step(m, carry):
            u, v = carry
            j = m + sweep
            wait_piece(sweep, j)
            cu, cv = unpack(sweep, j)
            u, v = coarse(u, v, maps[0], maps[1])
            u, v = u + cu, v + cv
            made[sweep, m, 0] = u[:, :LANES]
            made[sweep, m, 1] = v[:, :LANES]
            send_state(sweep, m + 1, made.at[sweep, m])
            return u, v

        lax.fori_loop(1, NTS - 1, step, (u, v))
        if sweep == 0:
            def over(k, carry):
                send_over(k + 1, made.at[0, k])
                return carry

            lax.fori_loop(0, NTS - 1, over, 0)

    @pl.when(jnp.logical_not(last))
    def _():
        propagate(0)

    @pl.when(last)
    def _():
        for i in range(HALO - 1):
            take_class(i)

    relay(0)

    def wait_plane(sweep, p):
        if sweep == 0:
            ref = lv.at[4, HALO + p]
        else:
            ref = out.at[0, :, p]
        pltpu.make_async_copy(ref, ref, vr.at[sweep, p]).wait()

    @pl.when(t > 0)
    def _():
        wait_plane(0, PLANES - 1)
        wait_plane(0, 0)
        send_planes((0, 3))
        wait_plane(0, 1)
        wait_plane(0, 2)
        send_planes((1, 2))
        propagate(1)

    @pl.when(t == 0)
    def _():
        drain_first()

    @pl.when(end)
    def _():
        arrived(made.at[0, pl.ds(0, NTS - 1)], es)

    relay(1)

    @pl.when(t > 0)
    def _():
        drain_planes()
        drain_pieces(1)

    @pl.when(t > 1)
    def _():
        for p in range(PLANES):
            wait_plane(1, p)

    drain_states(1)


def on_device(slice_starts, class_map, table):
    field, dma = (2, ROWS, COLS), pltpu.SemaphoreType.DMA
    return pl.pallas_call(
        kernel,
        out_shape=pltpu.VMEM(slice_starts.shape, jnp.float32),
        in_specs=[
            pl.BlockSpec(memory_space=pl.ANY),
            pl.BlockSpec(memory_space=pl.ANY),
            pl.BlockSpec(memory_space=pltpu.SMEM),
        ],
        out_specs=pl.BlockSpec(memory_space=pltpu.VMEM),
        scratch_shapes=[
            pltpu.VMEM((2 * FINE, DEEP) + field, jnp.float32),
            pltpu.VMEM((DEEP, ROWS, COLS), jnp.int32),
            pltpu.VMEM((DEEP,) + field, jnp.float32),
            pltpu.VMEM((PLANES,) + field, jnp.float32),
            pltpu.VMEM((2, NTS, PIECE, LANES), jnp.float32),
            pltpu.VMEM((2, NTS, PIECE, LANES), jnp.float32),
            pltpu.VMEM((2, NTS, 2, ROWS, LANES), jnp.float32),
            pltpu.VMEM((len(ROUND), ROWS, COLS), jnp.float32),
            pltpu.VMEM((HALO, 2, ROWS, COLS), jnp.float32),
            pltpu.VMEM((len(LATE), ROWS, COLS), jnp.float32),
            pltpu.VMEM((HALO - 1, ROWS, COLS), jnp.int32),
            pltpu.VMEM((HALO - NEAR,) + field, jnp.float32),
            dma((PLANES + 1,)),
            dma((2,)),
            dma((2, HALO, 2)),
            dma,
            dma((len(ROUND),)),
            dma,
            dma((len(LATE),)),
            dma,
            dma((HALO, 2)),
            dma((2,)),
            dma((2, HALO - 1)),
            dma((2,)),
            dma((2, HALO - 1)),
            dma,
            dma((HALO - 1,)),
            dma((2,)),
            dma((2, HALO)),
            dma,
            dma((HALO - NEAR,)),
            dma,
            dma((2,)),
            dma((2, NTS)),
            dma((2,)),
            dma((2, PLANES)),
            pltpu.SemaphoreType.REGULAR,
            pltpu.SemaphoreType.REGULAR,
        ],
        compiler_params=pltpu.CompilerParams(
            collective_id=0, has_side_effects=True, vmem_limit_bytes=60 * 1024 * 1024
        ),
        name="parareal",
    )(slice_starts, class_map, table.T)


def solution(mesh):
    in_specs = (P("tm", None, "slab", None, None), P("slab", None, None), P())
    out_specs = P("tm", None, "slab", None, None)
    return jax.shard_map(
        on_device, mesh=mesh, in_specs=in_specs, out_specs=out_specs, check_vma=False
    )
```

```python
import functools

import jax
import jax.numpy as jnp
from jax import lax
from jax.experimental import pallas as pl
from jax.experimental.pallas import tpu as pltpu
from jax.sharding import PartitionSpec as P

FINE = 4
CLASSES = 4
NTS = 16
FEED = 0.04
KILL = 0.062
STEP = 0.04
PLANES = 4
ROWS = 16
COLS = 512
LANES = 128
CHUNKS = COLS // LANES
HALO = FINE
DEEP = PLANES + 2 * HALO
PIECE = 2 * ROWS + 8
MESH = pl.DeviceIdType.MESH
TALL = 8
ROUND = ((3, 0), (3, 1), (2, 1))
NEAR = 2
LATE = ((3, 0), (3, 1))


def react(u, v, scale):
    uvv = u * v * v
    return scale * (FEED * (1.0 - u) - uvv), scale * (uvv - (FEED + KILL) * v)


def four(a):
    rows, cols = a.shape
    return (
        pltpu.roll(a, 1, 1)
        + pltpu.roll(a, cols - 1, 1)
        + pltpu.roll(a, 1, 0)
        + pltpu.roll(a, rows - 1, 0)
    )


def coarse(u, v, cu, cv):
    ru, rv = react(u, v, FINE * STEP)
    return u + cu * (four(u) - 4.0 * u) + ru, v + cv * (four(v) - 4.0 * v) + rv


def coarse_of(lam):
    return FINE * lam / (1.0 + 4.0 * FINE * lam)


def kernel(
    ss, cm_in, table, out,
    lv, cm, lam, gb, pack, got, made, tails, heads, late, kinds, planes,
    load_sem, hs, hr, ts, tr, ls, lr, ds, dr, cs, cr, xs, xr, ks, kr,
    gs, gr, es, er, fs, ps, pr, vs, vr, ready, here,
):
    t = lax.axis_index("tm")
    s = lax.axis_index("slab")
    slabs = lax.axis_size("slab")
    up = lax.rem(s + 1, slabs)
    down = lax.rem(s + slabs - 1, slabs)
    my_plane = lax.rem(t, PLANES)
    my_chunk = t // PLANES
    my_columns = pl.ds(pl.multiple_of(my_chunk * LANES, LANES), LANES)
    core = lax.rem(t, 2)
    partner = t + 1 - 2 * core
    last = t == NTS - 1
    height = lax.rem(s, TALL)
    top, bottom = height == TALL - 1, height == 0
    end = top | bottom
    across = jnp.where(top, s - (TALL - 1), jnp.where(bottom, s + (TALL - 1), s))
    beside_up = lax.rem(s + TALL, slabs)
    beside_down = lax.rem(s + slabs - TALL, slabs)
    UP, DOWN = 0, 1

    def signal(sem, where):
        pl.semaphore_signal(sem, inc=1, device_id=where, device_id_type=MESH)

    def remote(src, dst, send, recv, where):
        return pltpu.make_async_remote_copy(
            src_ref=src,
            dst_ref=dst,
            send_sem=send,
            recv_sem=recv,
            device_id=where,
            device_id_type=MESH,
        )

    def arrived(ref, sem):
        pltpu.make_async_copy(ref, ref, sem).wait()

    barrier = pltpu.get_barrier_semaphore()
    signal(barrier, (partner, s))
    signal(barrier, (t, down))

    @pl.when(jnp.logical_not(top))
    def _():
        signal(barrier, (t, up))

    @pl.when(bottom)
    def _():
        for z in (across, beside_up, beside_down):
            signal(barrier, (t, z))

    @pl.when(jnp.logical_not(last | end))
    def _():
        signal(barrier, (NTS - 1, s))

    loads = [
        pltpu.make_async_copy(ss.at[0, :, p], lv.at[0, HALO + p], load_sem.at[p])
        for p in range(PLANES)
    ]
    loads.append(pltpu.make_async_copy(cm_in, cm.at[pl.ds(HALO, PLANES)], load_sem.at[PLANES]))
    for copy in loads:
        copy.start()
    pl.semaphore_wait(barrier, 3 + jnp.where(end, 1, 0) + jnp.where(last, NTS - 1, 0))

    @pl.when(top)
    def _():
        signal(here, (t, up))
        signal(here, (t, across))

        @pl.when(jnp.logical_not(last))
        def _():
            signal(barrier, (NTS - 1, s))

    @pl.when(last)
    def _():
        @pl.when(bottom)
        def _():
            pl.semaphore_wait(here, 2)

        def tell(peer, carry):
            signal(ready, (peer, s))
            return carry

        lax.fori_loop(0, NTS - 1, tell, 0)

    def carrier(way):
        return ((core == way) & (t < NTS - 2)) | (t == NTS - 2)

    def class_planes(way, i):
        return (PLANES - 1 - i, HALO - 1 - i) if way == UP else (i, HALO + PLANES + i)

    def class_copy(way, i):
        src, plane = class_planes(way, i)
        return remote(
            cm_in.at[src], cm.at[plane], cs.at[way], cr.at[way, i], (t, down if way else up)
        )

    def kind_copy(i):
        return remote(cm_in.at[i], kinds.at[i], cs.at[DOWN], kr.at[i], (t, beside_down))

    def kind_forward(i):
        return remote(
            kinds.at[i], cm.at[HALO + PLANES + i], ks, cr.at[DOWN, i], (t, across)
        )

    def class_share(way, i):
        plane = class_planes(way, i)[1]
        return remote(cm.at[plane], cm.at[plane], xs.at[way], xr.at[way, i], (partner, s))

    def send_class():
        @pl.when(carrier(UP))
        def _():
            for i in range(HALO - 1):
                class_copy(UP, i).start()

        @pl.when(carrier(DOWN) & bottom)
        def _():
            for i in range(HALO - 1):
                kind_copy(i).start()

        @pl.when(carrier(DOWN) & jnp.logical_not(bottom))
        def _():
            for i in range(HALO - 1):
                class_copy(DOWN, i).start()

    def pass_class():
        @pl.when(carrier(DOWN))
        def _():
            for i in range(HALO - 1):
                copy = kind_forward(i)
                kind_copy(i).wait_recv()
                copy.start()

    def share_class():
        for way in (UP, DOWN):

            @pl.when(carrier(way))
            def _():
                for i in range(HALO - 1):
                    share = class_share(way, i)
                    class_copy(way, i).wait_recv()
                    share.start()

    def take_class(i):
        for way in (UP, DOWN):

            @pl.when(jnp.logical_not(carrier(way)))
            def _():
                class_share(way, i).wait_recv()

        diffusivity(HALO - 1 - i)
        diffusivity(HALO + PLANES + i)

    def drain_class():
        some = cm.at[pl.ds(0, HALO - 1)]
        for way in (UP, DOWN):

            @pl.when(carrier(way))
            def _():
                arrived(some, cs.at[way])
                arrived(some, xs.at[way])

        @pl.when(bottom & carrier(DOWN))
        def _():
            arrived(kinds, ks)

    def unit_source(way, i, field):
        return ss.at[0, field, PLANES - 1 - i if way == UP else i]

    def unit_target(way, i, field):
        return lv.at[0, HALO - 1 - i if way == UP else HALO + PLANES + i, field]

    def unit_copy(way, i, field):
        return remote(
            unit_source(way, i, field),
            unit_target(way, i, field),
            hs.at[way],
            hr.at[way, i, field],
            (t, up if way == UP else down),
        )

    def tail_copy(n):
        i, field = ROUND[n]
        return remote(
            unit_source(UP, i, field), tails.at[n], hs.at[UP], tr.at[n], (t, across)
        )

    def tail_forward(n):
        i, field = ROUND[n]
        return remote(
            tails.at[n], unit_target(UP, i, field), ts, hr.at[UP, i, field], (t, beside_up)
        )

    def head_copy(i, field):
        return remote(
            unit_source(DOWN, i, field),
            heads.at[i, field],
            hs.at[DOWN],
            dr.at[i, field],
            (t, beside_down),
        )

    def head_forward(i, field):
        return remote(
            heads.at[i, field],
            unit_target(DOWN, i, field),
            ds,
            hr.at[DOWN, i, field],
            (t, across),
        )

    def late_copy(n):
        i, field = LATE[n]
        return remote(
            unit_source(DOWN, i, field), late.at[n], hs.at[DOWN], lr.at[n], (t, across)
        )

    def late_forward(n):
        i, field = LATE[n]
        return remote(
            late.at[n],
            unit_target(DOWN, i, field),
            ls,
            hr.at[DOWN, i, field],
            (t, beside_down),
        )

    UNITS = [(i, field) for i in range(HALO) for field in range(2)]
    EARLY = [unit for unit in UNITS if unit not in LATE]

    def send_tails():
        for n in range(len(ROUND)):
            tail_copy(n).start()

    def send_starts():
        @pl.when(top)
        def _():
            for i, field in UNITS:
                if (i, field) not in ROUND:
                    unit_copy(UP, i, field).start()
            for i, field in UNITS:
                unit_copy(DOWN, i, field).start()

        @pl.when(bottom)
        def _():
            for i, field in UNITS:
                if (i, field) in EARLY:
                    head_copy(i, field).start()
                unit_copy(UP, i, field).start()

        @pl.when(jnp.logical_not(end))
        def _():
            for i, field in UNITS:
                unit_copy(UP, i, field).start()
                unit_copy(DOWN, i, field).start()

    def pass_heads(units):
        for i, field in units:
            copy = head_forward(i, field)
            head_copy(i, field).wait_recv()
            copy.start()

    def pass_tails():
        for n in range(len(ROUND)):
            copy = tail_forward(n)
            tail_copy(n).wait_recv()
            copy.start()

    def pass_late():
        for n in range(len(LATE)):
            copy = late_forward(n)
            late_copy(n).wait_recv()
            copy.start()

    def drain_starts():
        for way in (UP, DOWN):
            arrived(lv.at[0, pl.ds(0, HALO)], hs.at[way])

        @pl.when(bottom)
        def _():
            arrived(heads.at[pl.ds(0, len(EARLY) // 2)], ds)
            arrived(tails, ts)

        @pl.when(top)
        def _():
            arrived(late, ls)

    def outer(way, i):
        return lv.at[4, HALO - 1 - i if way == UP else HALO + PLANES + i]

    def plane_copy(way, i):
        return remote(
            lv.at[4, HALO + (PLANES - 1 - i if way == UP else i)],
            outer(way, i),
            gs.at[way],
            gr.at[way, i],
            (t, up if way == UP else down),
        )

    def send_planes(each):
        for way, over in ((UP, top), (DOWN, bottom)):

            @pl.when(jnp.logical_not(over))
            def _():
                for i in each:
                    plane_copy(way, i).start()

    def plane_forward(i):
        n = i - NEAR
        return remote(
            planes.at[n],
            lv.at[4, jnp.where(bottom, HALO - 1 - i, HALO + PLANES + i)],
            fs,
            gr.at[jnp.where(bottom, UP, DOWN), i],
            (t, jnp.where(bottom, beside_up, beside_down)),
        )

    def pass_planes():
        @pl.when(end)
        def _():
            for i in range(NEAR, HALO):
                n = i - NEAR
                copy = plane_forward(i)
                arrived(planes.at[n], er.at[n])
                copy.start()

    def drain_planes():
        for way, over in ((UP, top), (DOWN, bottom)):

            @pl.when(jnp.logical_not(over))
            def _():
                arrived(lv.at[4, pl.ds(0, HALO)], gs.at[way])

        @pl.when(end)
        def _():
            arrived(planes, fs)

    far = jnp.where(top, PLANES - 1 - my_plane, my_plane)

    def straight_copy(target, src):
        return remote(
            src,
            lv.at[4, jnp.where(top, my_plane, HALO + PLANES + my_plane), :, :, my_columns],
            es,
            gr.at[jnp.where(top, UP, DOWN), far],
            (target, jnp.where(top, up, down)),
        )

    def round_copy(target, src):
        n = jnp.where(far < NEAR, 0, far - NEAR)
        return remote(
            src, planes.at[n, :, :, my_columns], es, er.at[n], (target, across)
        )

    def send_over(where):
        for there, copy in ((far < NEAR, straight_copy), (far >= NEAR, round_copy)):

            @pl.when(where & there)
            def _():
                def one(k, carry):
                    copy(k + 1, made.at[0, k]).start()
                    return carry

                lax.fori_loop(0, NTS - 1, one, 0)

    def wait_side(sweep, i, side):
        plane = jnp.where(side == UP, HALO - 1 - i, HALO + PLANES + i)
        if sweep == 0:
            for field in range(2):
                arrived(lv.at[0, plane, field], hr.at[side, i, field])
        else:
            arrived(lv.at[4, plane], gr.at[side, i])

    @pl.when(top & jnp.logical_not(last))
    def _():
        send_tails()

    send_class()

    @pl.when(jnp.logical_not(last))
    def _():
        send_starts()

    def diffusivity(plane):
        klass = cm[plane]
        for field in range(2):
            value = jnp.zeros(klass.shape, jnp.float32)
            for k in range(CLASSES):
                value = jnp.where(klass == k, table[field, k], value)
            lam[plane, field] = value

    for copy in loads:
        copy.wait()

    def own_lam(p, carry):
        diffusivity(HALO + p)
        return carry

    lax.fori_loop(0, PLANES, own_lam, 0)

    def fine(base, level, plane):
        u, v = lv[base + level - 1, plane, 0], lv[base + level - 1, plane, 1]
        lap_u = lv[base + level - 1, plane - 1, 0] + lv[base + level - 1, plane + 1, 0]
        lap_v = lv[base + level - 1, plane - 1, 1] + lv[base + level - 1, plane + 1, 1]
        lap_u = lap_u + four(u) - 6.0 * u
        lap_v = lap_v + four(v) - 6.0 * v
        ru, rv = react(u, v, STEP)
        return u + lam[plane, 0] * lap_u + ru, v + lam[plane, 1] * lap_v + rv

    def fine_side(base, d, side):
        def step(k, carry):
            low = HALO - d + k
            plane = jnp.where(side == UP, low, DEEP - 1 - low)
            u, v = fine(base, k, plane)
            lv[base + k, plane, 0] = u
            lv[base + k, plane, 1] = v
            return carry

        lax.fori_loop(1, min(d + 1, FINE - 1) + 1, step, 0)

    def fine_inside(base):
        for plane in (HALO + 1, HALO + 2):
            u, v = fine(base, 1, plane)
            lv[base + 1, plane, 0] = u
            lv[base + 1, plane, 1] = v

    def guesses(sweep):
        keep = jnp.where(t == sweep, 0.0, 1.0).astype(jnp.float32)

        def one(p, carry):
            q = HALO + p
            cu, cv = coarse_of(lam[q, 0]), coarse_of(lam[q, 1])
            gu, gv = coarse(lv[4 * sweep, q, 0], lv[4 * sweep, q, 1], cu, cv)
            gb[p, 0] = keep * gu
            gb[p, 1] = keep * gv
            return carry

        lax.fori_loop(0, PLANES, one, 0)

    def piece_copy(sweep, owner):
        return pltpu.make_async_remote_copy(
            src_ref=pack.at[sweep, owner],
            dst_ref=got.at[sweep, t],
            send_sem=ps.at[sweep],
            recv_sem=pr.at[sweep, t],
            device_id=(owner, s),
            device_id_type=MESH,
        )

    lane = lax.broadcasted_iota(jnp.int32, (8, LANES), 1)

    def last_step(sweep, q):
        p = q - HALO
        u, v = fine(4 * sweep, FINE, q)
        @pl.when(t == sweep)
        def _():
            out[0, 0, p] = u
            out[0, 1, p] = v
        u = u - gb[p, 0]
        v = v - gb[p, 1]
        for c in range(CHUNKS):
            owner = c * PLANES + p
            here = slice(c * LANES, (c + 1) * LANES)
            after = ((c + 1) % CHUNKS) * LANES
            before = ((c - 1) % CHUNKS) * LANES
            pack[sweep, owner, 0:ROWS] = u[:, here]
            pack[sweep, owner, ROWS : 2 * ROWS] = v[:, here]
            edges = None
            for quarter, (field, row) in enumerate(((u, 0), (u, 8), (v, 0), (v, 8))):
                both = jnp.where(
                    lane < 64,
                    field[row : row + 8, after : after + LANES],
                    field[row : row + 8, before : before + LANES],
                )
                both = pltpu.roll(both, 32 * quarter + 16, 1)
                edges = both if edges is None else jnp.where(lane // 32 == quarter, both, edges)
            pack[sweep, owner, 2 * ROWS : PIECE] = edges

        def send(k, carry):
            owner = lax.rem(my_chunk + CHUNKS + 2 - k, CHUNKS) * PLANES + p

            @pl.when(owner != t)
            def _():
                piece_copy(sweep, owner).start()

            @pl.when(owner == t)
            def _():
                pltpu.make_async_copy(
                    pack.at[sweep, owner], got.at[sweep, t], pr.at[sweep, t]
                ).start()

            return carry

        lax.fori_loop(0, CHUNKS, send, 0)

    def propagate(sweep):
        base = 4 * sweep
        if sweep == 1:
            pass_planes()
        fine_inside(base)
        guesses(sweep)
        if sweep == 0:
            @pl.when(bottom)
            def _():
                pl.semaphore_wait(here, 2)
                signal(barrier, (NTS - 1, s))
                for n in range(len(LATE)):
                    late_copy(n).start()
                pass_class()
                pass_heads(EARLY[:2])
                pass_tails()
                pass_heads(EARLY[2:])

            share_class()

            @pl.when(top)
            def _():
                pass_late()

        if sweep == 1:
            drain_first()
        for d in range(1, HALO + 1):
            if sweep == 0 and d >= 2:
                take_class(d - 2)
            for turn in range(2):
                side = jnp.where(top, turn, 1 - turn)
                wait_side(sweep, d - 1, side)
                fine_side(base, d, side)
                if d + 1 >= FINE:
                    if sweep == 0 and d + 1 == FINE and turn == 0:
                        pl.semaphore_wait(ready, 1)
                    low = 2 * HALO - d
                    last_step(sweep, jnp.where(side == UP, low, DEEP - 1 - low))

    def state_copy(sweep, target, src):
        if sweep == 0:
            dst = lv.at[4, HALO + my_plane, :, :, my_columns]
        else:
            dst = out.at[0, :, my_plane, :, my_columns]
        return (
            pltpu.make_async_remote_copy(
                src_ref=src,
                dst_ref=dst,
                send_sem=vs.at[sweep],
                recv_sem=vr.at[sweep, my_plane],
                device_id=(target, s),
                device_id_type=MESH,
            ),
            pltpu.make_async_copy(src, dst, vr.at[sweep, my_plane]),
        )

    def send_state(sweep, target, src):
        there, local = state_copy(sweep, target, src)

        @pl.when(target != t)
        def _():
            there.start()

        @pl.when(target == t)
        def _():
            local.start()


    def drain_pieces(sweep):
        arrived(pack.at[sweep, pl.ds(0, NTS - 1)], ps.at[sweep])

    def drain_states(sweep):
        for own in (0, 1):

            @pl.when((t > sweep) == bool(own))
            def _():
                arrived(made.at[sweep, pl.ds(0, NTS - 1 - sweep - own)], vs.at[sweep])

    def drain_first():
        drain_class()

        @pl.when(jnp.logical_not(last))
        def _():
            drain_starts()
            drain_pieces(0)

        drain_states(0)

    def wait_piece(sweep, j):
        pltpu.make_async_copy(got.at[sweep, j], got.at[sweep, j], pr.at[sweep, j]).wait()

    def unpack(sweep, j):
        edges = got[sweep, j, 2 * ROWS : PIECE]
        parts = [pltpu.roll(edges, LANES - (32 * quarter + 16), 1) for quarter in range(4)]
        fields = []
        for field in range(2):
            side = jnp.concatenate(parts[2 * field : 2 * field + 2], axis=0)
            main = got[sweep, j, field * ROWS : (field + 1) * ROWS]
            fields.append(jnp.concatenate([main, side], axis=1))
        return fields

    def relay(sweep):
        columns = [
            pl.ds(pl.multiple_of(lax.rem(my_chunk + k, CHUNKS) * LANES, LANES), LANES)
            for k in (0, 1, CHUNKS - 1)
        ]
        wide = lax.broadcasted_iota(jnp.int32, (ROWS, LANES), 1)
        maps = []
        for field in range(2):
            here, after, before = [lam[HALO + my_plane, field, :, c] for c in columns]
            both = jnp.concatenate([here, jnp.where(wide < 64, after, before)], axis=1)
            maps.append(coarse_of(both))
        wait_piece(sweep, sweep)
        u, v = unpack(sweep, sweep)
        if sweep == 0:
            made[0, 0, 0] = u[:, :LANES]
            made[0, 0, 1] = v[:, :LANES]
            send_state(0, 1, made.at[0, 0])

        def step(m, carry):
            u, v = carry
            j = m + sweep
            wait_piece(sweep, j)
            cu, cv = unpack(sweep, j)
            u, v = coarse(u, v, maps[0], maps[1])
            u, v = u + cu, v + cv
            made[sweep, m, 0] = u[:, :LANES]
            made[sweep, m, 1] = v[:, :LANES]
            send_state(sweep, m + 1, made.at[sweep, m])
            return u, v

        lax.fori_loop(1, NTS - 1, step, (u, v))
        if sweep == 0:
            send_over(top)

    @pl.when(jnp.logical_not(last))
    def _():
        propagate(0)

    @pl.when(last)
    def _():
        for i in range(HALO - 1):
            take_class(i)

    relay(0)

    def wait_plane(sweep, p):
        if sweep == 0:
            ref = lv.at[4, HALO + p]
        else:
            ref = out.at[0, :, p]
        pltpu.make_async_copy(ref, ref, vr.at[sweep, p]).wait()

    @pl.when(t > 0)
    def _():
        for p in range(PLANES):
            wait_plane(0, p)
        send_planes(range(HALO))
        send_over(bottom)
        propagate(1)

    @pl.when(t == 0)
    def _():
        send_over(bottom)
        drain_first()

    @pl.when(end)
    def _():
        arrived(made.at[0, pl.ds(0, NTS - 1)], es)

    relay(1)

    @pl.when(t > 0)
    def _():
        drain_planes()
        drain_pieces(1)

    @pl.when(t > 1)
    def _():
        for p in range(PLANES):
            wait_plane(1, p)

    drain_states(1)


def on_device(slice_starts, class_map, table):
    field, dma = (2, ROWS, COLS), pltpu.SemaphoreType.DMA
    return pl.pallas_call(
        kernel,
        out_shape=pltpu.VMEM(slice_starts.shape, jnp.float32),
        in_specs=[
            pl.BlockSpec(memory_space=pl.ANY),
            pl.BlockSpec(memory_space=pl.ANY),
            pl.BlockSpec(memory_space=pltpu.SMEM),
        ],
        out_specs=pl.BlockSpec(memory_space=pltpu.VMEM),
        scratch_shapes=[
            pltpu.VMEM((2 * FINE, DEEP) + field, jnp.float32),
            pltpu.VMEM((DEEP, ROWS, COLS), jnp.int32),
            pltpu.VMEM((DEEP,) + field, jnp.float32),
            pltpu.VMEM((PLANES,) + field, jnp.float32),
            pltpu.VMEM((2, NTS, PIECE, LANES), jnp.float32),
            pltpu.VMEM((2, NTS, PIECE, LANES), jnp.float32),
            pltpu.VMEM((2, NTS, 2, ROWS, LANES), jnp.float32),
            pltpu.VMEM((len(ROUND), ROWS, COLS), jnp.float32),
            pltpu.VMEM((HALO, 2, ROWS, COLS), jnp.float32),
            pltpu.VMEM((len(LATE), ROWS, COLS), jnp.float32),
            pltpu.VMEM((HALO - 1, ROWS, COLS), jnp.int32),
            pltpu.VMEM((HALO - NEAR,) + field, jnp.float32),
            dma((PLANES + 1,)),
            dma((2,)),
            dma((2, HALO, 2)),
            dma,
            dma((len(ROUND),)),
            dma,
            dma((len(LATE),)),
            dma,
            dma((HALO, 2)),
            dma((2,)),
            dma((2, HALO - 1)),
            dma((2,)),
            dma((2, HALO - 1)),
            dma,
            dma((HALO - 1,)),
            dma((2,)),
            dma((2, HALO)),
            dma,
            dma((HALO - NEAR,)),
            dma,
            dma((2,)),
            dma((2, NTS)),
            dma((2,)),
            dma((2, PLANES)),
            pltpu.SemaphoreType.REGULAR,
            pltpu.SemaphoreType.REGULAR,
        ],
        compiler_params=pltpu.CompilerParams(
            collective_id=0, has_side_effects=True, vmem_limit_bytes=60 * 1024 * 1024
        ),
        name="parareal",
    )(slice_starts, class_map, table.T)


def solution(mesh):
    in_specs = (P("tm", None, "slab", None, None), P("slab", None, None), P())
    out_specs = P("tm", None, "slab", None, None)
    return jax.shard_map(
        on_device, mesh=mesh, in_specs=in_specs, out_specs=out_specs, check_vma=False
    )
```

```python
import functools

import jax
import jax.numpy as jnp
from jax import lax
from jax.experimental import pallas as pl
from jax.experimental.pallas import tpu as pltpu
from jax.sharding import PartitionSpec as P

FINE = 4
CLASSES = 4
NTS = 16
FEED = 0.04
KILL = 0.062
STEP = 0.04
PLANES = 4
ROWS = 16
COLS = 512
LANES = 128
CHUNKS = COLS // LANES
HALO = FINE
DEEP = PLANES + 2 * HALO
PIECE = 2 * ROWS + 8
MESH = pl.DeviceIdType.MESH
TALL = 8
ROUND = ((3, 0), (3, 1), (2, 1))
NEAR = 2
LATE = ((3, 0), (3, 1))


def react(u, v, scale):
    uvv = u * v * v
    return scale * (FEED * (1.0 - u) - uvv), scale * (uvv - (FEED + KILL) * v)


def four(a):
    rows, cols = a.shape
    return (
        pltpu.roll(a, 1, 1)
        + pltpu.roll(a, cols - 1, 1)
        + pltpu.roll(a, 1, 0)
        + pltpu.roll(a, rows - 1, 0)
    )


def coarse(u, v, cu, cv):
    ru, rv = react(u, v, FINE * STEP)
    return u + cu * (four(u) - 4.0 * u) + ru, v + cv * (four(v) - 4.0 * v) + rv


def coarse_of(lam):
    return FINE * lam / (1.0 + 4.0 * FINE * lam)


def kernel(
    ss, cm_in, table, out,
    lv, cm, lam, gb, pack, got, made, tails, heads, late, kinds, planes,
    load_sem, hs, hr, ts, tr, ls, lr, ds, dr, cs, cr, xs, xr, ks, kr,
    gs, gr, es, er, fs, ps, pr, vs, vr, ready, here,
):
    t = lax.axis_index("tm")
    s = lax.axis_index("slab")
    slabs = lax.axis_size("slab")
    up = lax.rem(s + 1, slabs)
    down = lax.rem(s + slabs - 1, slabs)
    my_plane = lax.rem(t, PLANES)
    my_chunk = t // PLANES
    my_columns = pl.ds(pl.multiple_of(my_chunk * LANES, LANES), LANES)
    core = lax.rem(t, 2)
    partner = t + 1 - 2 * core
    last = t == NTS - 1
    height = lax.rem(s, TALL)
    top, bottom = height == TALL - 1, height == 0
    end = top | bottom
    across = jnp.where(top, s - (TALL - 1), jnp.where(bottom, s + (TALL - 1), s))
    beside_up = lax.rem(s + TALL, slabs)
    beside_down = lax.rem(s + slabs - TALL, slabs)
    UP, DOWN = 0, 1

    def signal(sem, where):
        pl.semaphore_signal(sem, inc=1, device_id=where, device_id_type=MESH)

    def remote(src, dst, send, recv, where):
        return pltpu.make_async_remote_copy(
            src_ref=src,
            dst_ref=dst,
            send_sem=send,
            recv_sem=recv,
            device_id=where,
            device_id_type=MESH,
        )

    def arrived(ref, sem):
        pltpu.make_async_copy(ref, ref, sem).wait()

    barrier = pltpu.get_barrier_semaphore()
    signal(barrier, (partner, s))
    signal(barrier, (t, down))

    @pl.when(jnp.logical_not(top))
    def _():
        signal(barrier, (t, up))

    @pl.when(bottom)
    def _():
        for z in (across, beside_up, beside_down):
            signal(barrier, (t, z))

    @pl.when(jnp.logical_not(last | end))
    def _():
        signal(barrier, (NTS - 1, s))

    loads = [
        pltpu.make_async_copy(ss.at[0, :, p], lv.at[0, HALO + p], load_sem.at[p])
        for p in range(PLANES)
    ]
    loads.append(pltpu.make_async_copy(cm_in, cm.at[pl.ds(HALO, PLANES)], load_sem.at[PLANES]))
    for copy in loads:
        copy.start()
    pl.semaphore_wait(barrier, 3 + jnp.where(end, 1, 0) + jnp.where(last, NTS - 1, 0))

    @pl.when(top)
    def _():
        signal(here, (t, up))
        signal(here, (t, across))

        @pl.when(jnp.logical_not(last))
        def _():
            signal(barrier, (NTS - 1, s))

    @pl.when(last)
    def _():
        @pl.when(bottom)
        def _():
            pl.semaphore_wait(here, 2)

        def tell(peer, carry):
            signal(ready, (peer, s))
            return carry

        lax.fori_loop(0, NTS - 1, tell, 0)

    def carrier(way):
        return ((core == way) & (t < NTS - 2)) | (t == NTS - 2)

    def class_planes(way, i):
        return (PLANES - 1 - i, HALO - 1 - i) if way == UP else (i, HALO + PLANES + i)

    def class_copy(way, i):
        src, plane = class_planes(way, i)
        return remote(
            cm_in.at[src], cm.at[plane], cs.at[way], cr.at[way, i], (t, down if way else up)
        )

    def kind_copy(i):
        return remote(cm_in.at[i], kinds.at[i], cs.at[DOWN], kr.at[i], (t, beside_down))

    def kind_forward(i):
        return remote(
            kinds.at[i], cm.at[HALO + PLANES + i], ks, cr.at[DOWN, i], (t, across)
        )

    def class_share(way, i):
        plane = class_planes(way, i)[1]
        return remote(cm.at[plane], cm.at[plane], xs.at[way], xr.at[way, i], (partner, s))

    def send_class():
        @pl.when(carrier(UP))
        def _():
            for i in range(HALO - 1):
                class_copy(UP, i).start()

        @pl.when(carrier(DOWN) & bottom)
        def _():
            for i in range(HALO - 1):
                kind_copy(i).start()

        @pl.when(carrier(DOWN) & jnp.logical_not(bottom))
        def _():
            for i in range(HALO - 1):
                class_copy(DOWN, i).start()

    def pass_class():
        @pl.when(carrier(DOWN))
        def _():
            for i in range(HALO - 1):
                copy = kind_forward(i)
                kind_copy(i).wait_recv()
                copy.start()

    def share_class():
        for way in (UP, DOWN):

            @pl.when(carrier(way))
            def _():
                for i in range(HALO - 1):
                    share = class_share(way, i)
                    class_copy(way, i).wait_recv()
                    share.start()

    def take_class(i):
        for way in (UP, DOWN):

            @pl.when(jnp.logical_not(carrier(way)))
            def _():
                class_share(way, i).wait_recv()

        diffusivity(HALO - 1 - i)
        diffusivity(HALO + PLANES + i)

    def drain_class():
        some = cm.at[pl.ds(0, HALO - 1)]
        for way in (UP, DOWN):

            @pl.when(carrier(way))
            def _():
                arrived(some, cs.at[way])
                arrived(some, xs.at[way])

        @pl.when(bottom & carrier(DOWN))
        def _():
            arrived(kinds, ks)

    def unit_source(way, i, field):
        return ss.at[0, field, PLANES - 1 - i if way == UP else i]

    def unit_target(way, i, field):
        return lv.at[0, HALO - 1 - i if way == UP else HALO + PLANES + i, field]

    def unit_copy(way, i, field):
        return remote(
            unit_source(way, i, field),
            unit_target(way, i, field),
            hs.at[way],
            hr.at[way, i, field],
            (t, up if way == UP else down),
        )

    def tail_copy(n):
        i, field = ROUND[n]
        return remote(
            unit_source(UP, i, field), tails.at[n], hs.at[UP], tr.at[n], (t, across)
        )

    def tail_forward(n):
        i, field = ROUND[n]
        return remote(
            tails.at[n], unit_target(UP, i, field), ts, hr.at[UP, i, field], (t, beside_up)
        )

    def head_copy(i, field):
        return remote(
            unit_source(DOWN, i, field),
            heads.at[i, field],
            hs.at[DOWN],
            dr.at[i, field],
            (t, beside_down),
        )

    def head_forward(i, field):
        return remote(
            heads.at[i, field],
            unit_target(DOWN, i, field),
            ds,
            hr.at[DOWN, i, field],
            (t, across),
        )

    def late_copy(n):
        i, field = LATE[n]
        return remote(
            unit_source(DOWN, i, field), late.at[n], hs.at[DOWN], lr.at[n], (t, across)
        )

    def late_forward(n):
        i, field = LATE[n]
        return remote(
            late.at[n],
            unit_target(DOWN, i, field),
            ls,
            hr.at[DOWN, i, field],
            (t, beside_down),
        )

    UNITS = [(i, field) for i in range(HALO) for field in range(2)]
    EARLY = [unit for unit in UNITS if unit not in LATE]

    def send_tails():
        for n in range(len(ROUND)):
            tail_copy(n).start()

    def send_starts():
        @pl.when(top)
        def _():
            for i, field in UNITS:
                if (i, field) not in ROUND:
                    unit_copy(UP, i, field).start()
            for i, field in UNITS:
                unit_copy(DOWN, i, field).start()

        @pl.when(bottom)
        def _():
            for i, field in UNITS:
                if (i, field) in EARLY:
                    head_copy(i, field).start()
                unit_copy(UP, i, field).start()

        @pl.when(jnp.logical_not(end))
        def _():
            for i, field in UNITS:
                unit_copy(UP, i, field).start()
                unit_copy(DOWN, i, field).start()

    def pass_heads(units):
        for i, field in units:
            copy = head_forward(i, field)
            head_copy(i, field).wait_recv()
            copy.start()

    def pass_tails():
        for n in range(len(ROUND)):
            copy = tail_forward(n)
            tail_copy(n).wait_recv()
            copy.start()

    def pass_late():
        for n in range(len(LATE)):
            copy = late_forward(n)
            late_copy(n).wait_recv()
            copy.start()

    def drain_starts():
        for way in (UP, DOWN):
            arrived(lv.at[0, pl.ds(0, HALO)], hs.at[way])

        @pl.when(bottom)
        def _():
            arrived(heads.at[pl.ds(0, len(EARLY) // 2)], ds)
            arrived(tails, ts)

        @pl.when(top)
        def _():
            arrived(late, ls)

    def outer(way, i):
        return lv.at[4, HALO - 1 - i if way == UP else HALO + PLANES + i]

    def plane_copy(way, i):
        return remote(
            lv.at[4, HALO + (PLANES - 1 - i if way == UP else i)],
            outer(way, i),
            gs.at[way],
            gr.at[way, i],
            (t, up if way == UP else down),
        )

    def send_planes(each):
        for way, over in ((UP, top), (DOWN, bottom)):

            @pl.when(jnp.logical_not(over))
            def _():
                for i in each:
                    plane_copy(way, i).start()

    def plane_forward(i):
        n = i - NEAR
        return remote(
            planes.at[n],
            lv.at[4, jnp.where(bottom, HALO - 1 - i, HALO + PLANES + i)],
            fs,
            gr.at[jnp.where(bottom, UP, DOWN), i],
            (t, jnp.where(bottom, beside_up, beside_down)),
        )

    def pass_planes():
        @pl.when(end)
        def _():
            for i in range(NEAR, HALO):
                n = i - NEAR
                copy = plane_forward(i)
                arrived(planes.at[n], er.at[n])
                copy.start()

    def drain_planes():
        for way, over in ((UP, top), (DOWN, bottom)):

            @pl.when(jnp.logical_not(over))
            def _():
                arrived(lv.at[4, pl.ds(0, HALO)], gs.at[way])

        @pl.when(end)
        def _():
            arrived(planes, fs)

    far = jnp.where(top, PLANES - 1 - my_plane, my_plane)

    def straight_copy(target, src):
        return remote(
            src,
            lv.at[4, jnp.where(top, my_plane, HALO + PLANES + my_plane), :, :, my_columns],
            es,
            gr.at[jnp.where(top, UP, DOWN), far],
            (target, jnp.where(top, up, down)),
        )

    def round_copy(target, src):
        n = jnp.where(far < NEAR, 0, far - NEAR)
        return remote(
            src, planes.at[n, :, :, my_columns], es, er.at[n], (target, across)
        )

    def send_over(where):
        for there, copy in ((far < NEAR, straight_copy), (far >= NEAR, round_copy)):

            @pl.when(where & there)
            def _():
                def one(k, carry):
                    copy(k + 1, made.at[0, k]).start()
                    return carry

                lax.fori_loop(0, NTS - 1, one, 0)

    def wait_side(sweep, i, side):
        plane = jnp.where(side == UP, HALO - 1 - i, HALO + PLANES + i)
        if sweep == 0:
            for field in range(2):
                arrived(lv.at[0, plane, field], hr.at[side, i, field])
        else:
            arrived(lv.at[4, plane], gr.at[side, i])

    @pl.when(top & jnp.logical_not(last))
    def _():
        send_tails()

    send_class()

    @pl.when(jnp.logical_not(last))
    def _():
        send_starts()

    def diffusivity(plane):
        klass = cm[plane]
        for field in range(2):
            value = jnp.zeros(klass.shape, jnp.float32)
            for k in range(CLASSES):
                value = jnp.where(klass == k, table[field, k], value)
            lam[plane, field] = value

    for copy in loads:
        copy.wait()

    def own_lam(p, carry):
        diffusivity(HALO + p)
        return carry

    lax.fori_loop(0, PLANES, own_lam, 0)

    def fine(base, level, plane):
        u, v = lv[base + level - 1, plane, 0], lv[base + level - 1, plane, 1]
        lap_u = lv[base + level - 1, plane - 1, 0] + lv[base + level - 1, plane + 1, 0]
        lap_v = lv[base + level - 1, plane - 1, 1] + lv[base + level - 1, plane + 1, 1]
        lap_u = lap_u + four(u) - 6.0 * u
        lap_v = lap_v + four(v) - 6.0 * v
        ru, rv = react(u, v, STEP)
        return u + lam[plane, 0] * lap_u + ru, v + lam[plane, 1] * lap_v + rv

    def fine_side(base, d, side):
        def step(k, carry):
            low = HALO - d + k
            plane = jnp.where(side == UP, low, DEEP - 1 - low)
            u, v = fine(base, k, plane)
            lv[base + k, plane, 0] = u
            lv[base + k, plane, 1] = v
            return carry

        lax.fori_loop(1, min(d + 1, FINE - 1) + 1, step, 0)

    def fine_inside(base):
        for plane in (HALO + 1, HALO + 2):
            u, v = fine(base, 1, plane)
            lv[base + 1, plane, 0] = u
            lv[base + 1, plane, 1] = v

    def guesses(sweep):
        keep = jnp.where(t == sweep, 0.0, 1.0).astype(jnp.float32)

        def one(p, carry):
            q = HALO + p
            cu, cv = coarse_of(lam[q, 0]), coarse_of(lam[q, 1])
            gu, gv = coarse(lv[4 * sweep, q, 0], lv[4 * sweep, q, 1], cu, cv)
            gb[p, 0] = keep * gu
            gb[p, 1] = keep * gv
            return carry

        lax.fori_loop(0, PLANES, one, 0)

    def piece_copy(sweep, owner):
        return pltpu.make_async_remote_copy(
            src_ref=pack.at[sweep, owner],
            dst_ref=got.at[sweep, t],
            send_sem=ps.at[sweep],
            recv_sem=pr.at[sweep, t],
            device_id=(owner, s),
            device_id_type=MESH,
        )

    lane = lax.broadcasted_iota(jnp.int32, (8, LANES), 1)

    def last_step(sweep, q):
        p = q - HALO
        u, v = fine(4 * sweep, FINE, q)
        @pl.when(t == sweep)
        def _():
            out[0, 0, p] = u
            out[0, 1, p] = v
        u = u - gb[p, 0]
        v = v - gb[p, 1]
        for c in range(CHUNKS):
            owner = c * PLANES + p
            here = slice(c * LANES, (c + 1) * LANES)
            after = ((c + 1) % CHUNKS) * LANES
            before = ((c - 1) % CHUNKS) * LANES
            pack[sweep, owner, 0:ROWS] = u[:, here]
            pack[sweep, owner, ROWS : 2 * ROWS] = v[:, here]
            edges = None
            for quarter, (field, row) in enumerate(((u, 0), (u, 8), (v, 0), (v, 8))):
                both = jnp.where(
                    lane < 64,
                    field[row : row + 8, after : after + LANES],
                    field[row : row + 8, before : before + LANES],
                )
                both = pltpu.roll(both, 32 * quarter + 16, 1)
                edges = both if edges is None else jnp.where(lane // 32 == quarter, both, edges)
            pack[sweep, owner, 2 * ROWS : PIECE] = edges

        def send(k, carry):
            owner = lax.rem(my_chunk + CHUNKS + 2 - k, CHUNKS) * PLANES + p

            @pl.when(owner != t)
            def _():
                piece_copy(sweep, owner).start()

            @pl.when(owner == t)
            def _():
                pltpu.make_async_copy(
                    pack.at[sweep, owner], got.at[sweep, t], pr.at[sweep, t]
                ).start()

            return carry

        lax.fori_loop(0, CHUNKS, send, 0)

    def propagate(sweep):
        base = 4 * sweep
        if sweep == 1:
            pass_planes()
        fine_inside(base)
        guesses(sweep)
        if sweep == 0:
            @pl.when(bottom)
            def _():
                pl.semaphore_wait(here, 2)
                signal(barrier, (NTS - 1, s))
                for n in range(len(LATE)):
                    late_copy(n).start()
                pass_class()
                pass_heads(EARLY[:3])
                pass_tails()
                pass_heads(EARLY[3:])

            share_class()

            @pl.when(top)
            def _():
                pass_late()

        if sweep == 1:
            drain_first()
        for d in range(1, HALO + 1):
            if sweep == 0 and d >= 2:
                take_class(d - 2)
            for turn in range(2):
                side = jnp.where(top, turn, 1 - turn)
                wait_side(sweep, d - 1, side)
                fine_side(base, d, side)
                if d + 1 >= FINE:
                    if sweep == 0 and d + 1 == FINE and turn == 0:
                        pl.semaphore_wait(ready, 1)
                    low = 2 * HALO - d
                    last_step(sweep, jnp.where(side == UP, low, DEEP - 1 - low))

    def state_copy(sweep, target, src):
        if sweep == 0:
            dst = lv.at[4, HALO + my_plane, :, :, my_columns]
        else:
            dst = out.at[0, :, my_plane, :, my_columns]
        return (
            pltpu.make_async_remote_copy(
                src_ref=src,
                dst_ref=dst,
                send_sem=vs.at[sweep],
                recv_sem=vr.at[sweep, my_plane],
                device_id=(target, s),
                device_id_type=MESH,
            ),
            pltpu.make_async_copy(src, dst, vr.at[sweep, my_plane]),
        )

    def send_state(sweep, target, src):
        there, local = state_copy(sweep, target, src)

        @pl.when(target != t)
        def _():
            there.start()

        @pl.when(target == t)
        def _():
            local.start()


    def drain_pieces(sweep):
        arrived(pack.at[sweep, pl.ds(0, NTS - 1)], ps.at[sweep])

    def drain_states(sweep):
        for own in (0, 1):

            @pl.when((t > sweep) == bool(own))
            def _():
                arrived(made.at[sweep, pl.ds(0, NTS - 1 - sweep - own)], vs.at[sweep])

    def drain_first():
        drain_class()

        @pl.when(jnp.logical_not(last))
        def _():
            drain_starts()
            drain_pieces(0)

        drain_states(0)

    def wait_piece(sweep, j):
        pltpu.make_async_copy(got.at[sweep, j], got.at[sweep, j], pr.at[sweep, j]).wait()

    def unpack(sweep, j):
        edges = got[sweep, j, 2 * ROWS : PIECE]
        parts = [pltpu.roll(edges, LANES - (32 * quarter + 16), 1) for quarter in range(4)]
        fields = []
        for field in range(2):
            side = jnp.concatenate(parts[2 * field : 2 * field + 2], axis=0)
            main = got[sweep, j, field * ROWS : (field + 1) * ROWS]
            fields.append(jnp.concatenate([main, side], axis=1))
        return fields

    def relay(sweep):
        columns = [
            pl.ds(pl.multiple_of(lax.rem(my_chunk + k, CHUNKS) * LANES, LANES), LANES)
            for k in (0, 1, CHUNKS - 1)
        ]
        wide = lax.broadcasted_iota(jnp.int32, (ROWS, LANES), 1)
        maps = []
        for field in range(2):
            here, after, before = [lam[HALO + my_plane, field, :, c] for c in columns]
            both = jnp.concatenate([here, jnp.where(wide < 64, after, before)], axis=1)
            maps.append(coarse_of(both))
        wait_piece(sweep, sweep)
        u, v = unpack(sweep, sweep)
        if sweep == 0:
            made[0, 0, 0] = u[:, :LANES]
            made[0, 0, 1] = v[:, :LANES]
            send_state(0, 1, made.at[0, 0])

        def step(m, carry):
            u, v = carry
            j = m + sweep
            wait_piece(sweep, j)
            cu, cv = unpack(sweep, j)
            u, v = coarse(u, v, maps[0], maps[1])
            u, v = u + cu, v + cv
            made[sweep, m, 0] = u[:, :LANES]
            made[sweep, m, 1] = v[:, :LANES]
            send_state(sweep, m + 1, made.at[sweep, m])
            return u, v

        lax.fori_loop(1, NTS - 1, step, (u, v))
        if sweep == 0:
            send_over(top)

    @pl.when(jnp.logical_not(last))
    def _():
        propagate(0)

    @pl.when(last)
    def _():
        for i in range(HALO - 1):
            take_class(i)

    relay(0)

    def wait_plane(sweep, p):
        if sweep == 0:
            ref = lv.at[4, HALO + p]
        else:
            ref = out.at[0, :, p]
        pltpu.make_async_copy(ref, ref, vr.at[sweep, p]).wait()

    @pl.when(t > 0)
    def _():
        for p in range(PLANES):
            wait_plane(0, p)
        send_planes(range(HALO))
        send_over(bottom)
        propagate(1)

    @pl.when(t == 0)
    def _():
        send_over(bottom)
        drain_first()

    @pl.when(end)
    def _():
        arrived(made.at[0, pl.ds(0, NTS - 1)], es)

    relay(1)

    @pl.when(t > 0)
    def _():
        drain_planes()
        drain_pieces(1)

    @pl.when(t > 1)
    def _():
        for p in range(PLANES):
            wait_plane(1, p)

    drain_states(1)


def on_device(slice_starts, class_map, table):
    field, dma = (2, ROWS, COLS), pltpu.SemaphoreType.DMA
    return pl.pallas_call(
        kernel,
        out_shape=pltpu.VMEM(slice_starts.shape, jnp.float32),
        in_specs=[
            pl.BlockSpec(memory_space=pl.ANY),
            pl.BlockSpec(memory_space=pl.ANY),
            pl.BlockSpec(memory_space=pltpu.SMEM),
        ],
        out_specs=pl.BlockSpec(memory_space=pltpu.VMEM),
        scratch_shapes=[
            pltpu.VMEM((2 * FINE, DEEP) + field, jnp.float32),
            pltpu.VMEM((DEEP, ROWS, COLS), jnp.int32),
            pltpu.VMEM((DEEP,) + field, jnp.float32),
            pltpu.VMEM((PLANES,) + field, jnp.float32),
            pltpu.VMEM((2, NTS, PIECE, LANES), jnp.float32),
            pltpu.VMEM((2, NTS, PIECE, LANES), jnp.float32),
            pltpu.VMEM((2, NTS, 2, ROWS, LANES), jnp.float32),
            pltpu.VMEM((len(ROUND), ROWS, COLS), jnp.float32),
            pltpu.VMEM((HALO, 2, ROWS, COLS), jnp.float32),
            pltpu.VMEM((len(LATE), ROWS, COLS), jnp.float32),
            pltpu.VMEM((HALO - 1, ROWS, COLS), jnp.int32),
            pltpu.VMEM((HALO - NEAR,) + field, jnp.float32),
            dma((PLANES + 1,)),
            dma((2,)),
            dma((2, HALO, 2)),
            dma,
            dma((len(ROUND),)),
            dma,
            dma((len(LATE),)),
            dma,
            dma((HALO, 2)),
            dma((2,)),
            dma((2, HALO - 1)),
            dma((2,)),
            dma((2, HALO - 1)),
            dma,
            dma((HALO - 1,)),
            dma((2,)),
            dma((2, HALO)),
            dma,
            dma((HALO - NEAR,)),
            dma,
            dma((2,)),
            dma((2, NTS)),
            dma((2,)),
            dma((2, PLANES)),
            pltpu.SemaphoreType.REGULAR,
            pltpu.SemaphoreType.REGULAR,
        ],
        compiler_params=pltpu.CompilerParams(
            collective_id=0, has_side_effects=True, vmem_limit_bytes=60 * 1024 * 1024
        ),
        name="parareal",
    )(slice_starts, class_map, table.T)


def solution(mesh):
    in_specs = (P("tm", None, "slab", None, None), P("slab", None, None), P())
    out_specs = P("tm", None, "slab", None, None)
    return jax.shard_map(
        on_device, mesh=mesh, in_specs=in_specs, out_specs=out_specs, check_vma=False
    )
```
